512 devices in a mesh: dp: 32 (over x, y, core), ctx: 16 (over z).
Axes of the slice: x: 4, y: 4, z: 16, core: 2. Of those that a mesh axis runs over, the one named last changes fastest.
Arguments:
- query_rows: bfloat16 [65536, 1024], P(('dp', 'ctx')), may hold values from -6 to 6
- key_rows: bfloat16 [65536, 1024], P(('dp', 'ctx')), may hold values from -6 to 6
- value_rows: bfloat16 [65536, 1024], P(('dp', 'ctx')), may hold values from -6 to 6
- gate_rows: bfloat16 [65536, 1024], P(('dp', 'ctx')), may hold values from -6 to 6
- out_grad: bfloat16 [65536, 1024], P(('dp', 'ctx')), may hold values from -24 to 24
- proj_weight: bfloat16 [1024, 1024], P(('dp', 'ctx')), may hold values from -0.1875 to 0.1875
- user_lengths: int32 [32, 4], P('dp'), may hold values from 1 to 1024, 2048 in all within a row
Outputs:
- query_grad: bfloat16 [65536, 1024], P(('dp', 'ctx'))
- key_grad: bfloat16 [65536, 1024], P(('dp', 'ctx'))
- value_grad: bfloat16 [65536, 1024], P(('dp', 'ctx'))
- gate_grad: bfloat16 [65536, 1024], P(('dp', 'ctx'))
- proj_grad: float32 [1024, 1024], P('dp')
The draws below stay inside these ranges and needn't reach their ends.
Inputs may be any that keep to these rules, and one draw needn't show every extreme that they name: `user_lengths`: each row sums to 2048; its largest entry is exactly 1024.
All inputs are finite; a program needn't handle non-finite values.
Results may differ from the reference program's by a relative error of at most 0.013.
Values may be sent and summed in bfloat16 or wider, within the bound.
No kernel may reach another device: no remote copies, remote signals or barrier semaphores. Data moves between devices by JAX's collectives and lax.ppermute only.
A program may use at most 128 MiB of HBM per device.

```python
import math
import jax
import jax.numpy as jnp
import numpy as np
from jax import lax

HEADS = 16
DH = 64
D = 1024
USERS = 4
GROUP = 2048
TOKENS = 65536
MOST_LEN = 1024
N_DP = 32


def strengthened(result, rng, source, target, blocks, factor):
    def block_of(axis_at):
        return (jnp.arange(result.shape[axis_at]) // (result.shape[axis_at] // blocks)).reshape((-1,) + (1,) * (result.ndim - 1 - axis_at))

    near = jax.random.permutation(rng, blocks)[block_of(target)]
    second = (block_of(target) + blocks // 2) % blocks
    return jnp.where((block_of(source) == near) | (block_of(source) == second), factor * result, result)


def levels(own_key, shape, shards, low, top_value):
    gain, own = 1.0, jax.random.fold_in(own_key, 6)
    for axis_at, blocks in shards:
        steps = jnp.exp(jax.random.uniform(jax.random.fold_in(own, axis_at), (blocks,), jnp.float32, low / len(shards), top_value / len(shards)))
        gain = gain * jnp.repeat(steps, shape[axis_at] // blocks).reshape([-1 if axis == axis_at else 1 for axis in range(len(shape))])
    return gain


def split_up(number_of, total, most, lean):
    loads = [(1 << 20) // math.isqrt(rank ** lean) + 1 for rank in range(2, number_of + 1)]
    rest, given = total - most - (number_of - 1), [1] * (number_of - 1)
    while rest > 0:
        free = [i for i in range(number_of - 1) if given[i] < most]
        whole, remaining = sum([loads[i] for i in free]), rest
        for i in free:
            more = min(most - given[i], max(1, remaining * loads[i] // whole), rest)
            given[i] = given[i] + more
            rest = rest - more
    return np.array([most] + given)


def uneven(rng, count, total, bound, slope):
    if count == 2:
        one = jax.random.randint(rng, (), max(1, total - bound), min(bound, total - 1) + 1)
        return jnp.stack([one, total - one])
    lengths = jnp.asarray(split_up(count, total, bound, slope), jnp.int32)
    pairs = (count - 1) // 2
    source_of, receiver = lengths[1:1 + 2 * pairs:2], lengths[2:2 + 2 * pairs:2]
    margin = jnp.minimum(source_of - 1, bound - receiver)
    passed = jax.random.randint(jax.random.fold_in(rng, 1), (pairs,), 0, 1 << 20) % (margin + 1)
    lengths = lengths.at[1:1 + 2 * pairs:2].set(source_of - passed).at[2:2 + 2 * pairs:2].set(receiver + passed)
    return lengths[jax.random.permutation(jax.random.fold_in(rng, 2), count)]


def noise(key, extent, deviation, reach, pieces=(), kind=jnp.bfloat16):
    values = jax.random.normal(key, extent, jnp.float32) * deviation
    if len(pieces) > 0:
        values = levels(key, extent, pieces, -0.22, 0.18) * values
    return jnp.clip(values, min=-reach, max=reach).astype(kind)


def gaussian_with(stream_key, extent, deviation, bound, split, heavy, kind=jnp.bfloat16):
    drawn = deviation * jax.random.normal(stream_key, extent, jnp.float32)
    if split:
        drawn = drawn * levels(stream_key, extent, split, -0.22, 0.18)
    return jnp.clip(strengthened(drawn, jax.random.fold_in(stream_key, 3), *heavy), -bound, bound).astype(kind)


def setup_inputs(seed: int = 0) -> dict:
    key_of = jax.random.split(jax.random.key(seed), 8)
    query_rows = noise(key_of[0], (TOKENS, D), 1.0, 6.0, ((0, 512),))
    key_rows = noise(key_of[1], (TOKENS, D), 1.0, 6.0, ((0, 512),))
    value_rows = noise(key_of[2], (TOKENS, D), 1.0, 6.0, ((0, 512),))
    gate_rows = noise(key_of[3], (TOKENS, D), 1.0, 6.0, ((0, 512),))
    out_grad = gaussian_with(key_of[4], (TOKENS, D), 1.0, 24.0, ((0, 512),), (0, 1, 512, 6.0))
    proj_weight = noise(key_of[5], (D, D), D ** -0.5, 0.1875, ((0, 512),))
    user_lengths = jax.vmap(lambda own: uneven(own, USERS, GROUP, MOST_LEN, 2))(jax.random.split(key_of[6], N_DP)).reshape((N_DP, USERS)).astype(jnp.int32)
    return dict(query_rows=query_rows, key_rows=key_rows, value_rows=value_rows, gate_rows=gate_rows, out_grad=out_grad, proj_weight=proj_weight, user_lengths=user_lengths)


def silu_slope(scores):
    sigmoid = jax.nn.sigmoid(scores)
    return sigmoid * (1.0 + scores * (1.0 - sigmoid))

def user_tables(lengths_row, group_size):
    lengths_row = lengths_row.astype(jnp.int32)
    ends = jnp.cumsum(lengths_row).astype(jnp.int32)
    starts = ends - lengths_row
    position = jnp.arange(group_size, dtype=jnp.int32)
    member = (position[:, None] >= starts[None, :]) & (position[:, None] < ends[None, :])
    user_ids = lax.optimization_barrier(jnp.sum((position[:, None] >= ends[None, :]).astype(jnp.int32), axis=1))
    inverse = lax.optimization_barrier(jnp.sum(jnp.where(member, 1.0 / lengths_row.astype(jnp.float32)[None, :], jnp.float32(0.0)), axis=1))
    return (user_ids, inverse.astype(jnp.float32))

def weight_table(user_ids, inverse, group_size):
    position = jnp.arange(group_size, dtype=jnp.int32)
    allowed = (user_ids[:, None] == user_ids[None, :]) & (position[None, :] <= position[:, None])
    return jnp.where(allowed, inverse[:, None], jnp.float32(0.0))

def head_forward(query, key_head, value, weight):
    scale = 1.0 / math.sqrt(DH)
    scores = jnp.dot(query, key_head.T, preferred_element_type=jnp.float32) * scale
    attn = (jax.nn.silu(scores) * weight).astype(jnp.bfloat16)
    return jnp.dot(attn, value, preferred_element_type=jnp.float32).astype(jnp.bfloat16)

def head_backward(query, key_head, value, grad_head, weight):
    scale = 1.0 / math.sqrt(DH)
    scores = jnp.dot(query, key_head.T, preferred_element_type=jnp.float32) * scale
    attn = (jax.nn.silu(scores) * weight).astype(jnp.bfloat16)
    value_grad = jnp.dot(attn.T, grad_head, preferred_element_type=jnp.float32).astype(jnp.bfloat16)
    attn_grad = jnp.dot(grad_head, value.T, preferred_element_type=jnp.float32)
    score_grad = (attn_grad * weight * silu_slope(scores) * scale).astype(jnp.bfloat16)
    query_grad = jnp.dot(score_grad, key_head, preferred_element_type=jnp.float32).astype(jnp.bfloat16)
    key_grad = jnp.dot(score_grad.T, query, preferred_element_type=jnp.float32).astype(jnp.bfloat16)
    return (query_grad, key_grad, value_grad)

def to_heads(array):
    return array.reshape(N_DP, GROUP, HEADS, DH).transpose(0, 2, 1, 3)

def from_heads(array):
    return array.transpose(0, 2, 1, 3).reshape(TOKENS, D)

def reference(query_rows, key_rows, value_rows, gate_rows, out_grad, proj_weight, user_lengths):

    def group_forward(packed):
        queries, keys_all, values, lengths_row = packed
        user_ids, inverse = user_tables(lengths_row, GROUP)
        weight = weight_table(user_ids, inverse, GROUP)
        return lax.map(lambda items: head_forward(items[0], items[1], items[2], weight), (queries, keys_all, values))
    attn_out = from_heads(lax.map(group_forward, (to_heads(query_rows), to_heads(key_rows), to_heads(value_rows), user_lengths)))
    centred = attn_out.astype(jnp.float32)
    centred = centred - lax.optimization_barrier(jnp.mean(centred, axis=1, keepdims=True))
    rstd = lax.rsqrt(lax.optimization_barrier(jnp.mean(centred * centred, axis=1, keepdims=True)) + 1e-05)
    normed = centred * rstd
    gates = gate_rows.astype(jnp.float32)
    gated = (normed * gates).astype(jnp.bfloat16)
    gated_grad = jnp.dot(out_grad, proj_weight.T, preferred_element_type=jnp.float32)
    gate_grad = (gated_grad * normed).astype(jnp.bfloat16)
    normed_grad = gated_grad * gates
    out_grad_attn = (normed_grad - lax.optimization_barrier(jnp.mean(normed_grad, axis=1, keepdims=True)) - normed * lax.optimization_barrier(jnp.mean(normed_grad * normed, axis=1, keepdims=True))) * rstd
    out_grad_attn = out_grad_attn.astype(jnp.bfloat16)
    proj_grad = jnp.dot(gated.T, out_grad, preferred_element_type=jnp.float32)

    def group_backward(packed):
        queries, keys_all, values, grads, lengths_row = packed
        user_ids, inverse = user_tables(lengths_row, GROUP)
        weight = weight_table(user_ids, inverse, GROUP)
        return lax.map(lambda items: head_backward(items[0], items[1], items[2], items[3], weight), (queries, keys_all, values, grads))
    query_grad, key_grad, value_grad = lax.map(group_backward, (to_heads(query_rows), to_heads(key_rows), to_heads(value_rows), to_heads(out_grad_attn), user_lengths))
    return (from_heads(query_grad), from_heads(key_grad), from_heads(value_grad), gate_grad, proj_grad)
```

```python
import functools
import math

import jax
import jax.numpy as jnp
from jax import lax
from jax.experimental import pallas as pl
from jax.experimental.pallas import tpu as pltpu
from jax.sharding import PartitionSpec as P

DH = 64
LANES = 128
TILE = 256
BF16 = jnp.bfloat16
F32 = jnp.float32
VMEM = pl.BlockSpec(memory_space=pltpu.VMEM)
SMEM = pl.BlockSpec(memory_space=pltpu.SMEM)
LIMIT = 48 * 1024 * 1024


def call(kernel, out_shape, in_specs, scratch=(), flops=0, nbytes=0):
    single = not isinstance(out_shape, (list, tuple))
    out_specs = VMEM if single else [VMEM] * len(out_shape)
    return pl.pallas_call(
        kernel,
        out_shape=out_shape,
        in_specs=in_specs,
        out_specs=out_specs,
        scratch_shapes=list(scratch),
        compiler_params=pltpu.CompilerParams(vmem_limit_bytes=LIMIT),
        cost_estimate=pl.CostEstimate(flops=flops, bytes_accessed=nbytes, transcendentals=0),
    )


def pack_kernel(q_ref, k_ref, v_ref, w_ref, first_ref, second_ref):
    heads = first_ref.shape[0]
    for pair in range(heads // 2):
        cols = slice(pair * 2 * DH, (pair + 1) * 2 * DH)
        q_t = q_ref[:, cols].T
        k_t = k_ref[:, cols].T
        v_t = v_ref[:, cols].T
        for half in range(2):
            rows = slice(half * DH, (half + 1) * DH)
            first_ref[2 * pair + half, 0:DH, :] = q_t[rows]
            first_ref[2 * pair + half, DH : 2 * DH, :] = k_t[rows]
            second_ref[2 * pair + half] = v_t[rows]
    for head in range(heads):
        first_ref[head, 2 * DH :, :] = w_ref[...]


def unpack_kernel(count, x_ref, *out_refs):
    heads = x_ref.shape[0]
    for pair in range(heads // 2):
        for i in range(count):
            rows = slice(i * DH, (i + 1) * DH)
            both = jnp.concatenate([x_ref[2 * pair, rows, :], x_ref[2 * pair + 1, rows, :]], axis=0)
            out_refs[i][:, pair * 2 * DH : (pair + 1) * 2 * DH] = both.T


def user_edges(len_ref):
    ends = []
    total = 0
    for i in range(len_ref.shape[1]):
        total = total + len_ref[0, i]
        ends.append(total)
    return ends


def user_start(position, ends):
    start = jnp.zeros_like(position)
    for end in ends[:-1]:
        start = jnp.where(position >= end, end, start)
    return start


def user_inverse(position, ends, len_ref):
    length = jnp.full(position.shape, len_ref[0, 0], jnp.int32)
    for i, end in enumerate(ends[:-1]):
        length = jnp.where(position >= end, len_ref[0, i + 1], length)
    return 1.0 / length.astype(F32)


def lane_pair(ref, block, rows):
    return jnp.concatenate([ref[2 * block, rows, :], ref[2 * block + 1, rows, :]], axis=1)


def tile_allowed(row_block, col_block, starts, positions):
    key_pos = col_block * TILE + lax.broadcasted_iota(jnp.int32, (TILE, TILE), 0)
    return (key_pos >= starts) & (key_pos <= positions)


def block_rows(row_block, ends):
    positions = row_block * TILE + lax.broadcasted_iota(jnp.int32, (1, TILE), 1)
    return positions, user_start(positions, ends)


def first_block(row_block, ends):
    return lax.div(user_start(row_block * TILE, ends), TILE)


def natural(source_ref, rows, target_ref):
    for block in range(target_ref.shape[0]):
        for half in range(2):
            target_ref[block, half * LANES : (half + 1) * LANES, :] = source_ref[
                2 * block + half, rows, :
            ].T


Q_ROWS = slice(0, DH)
K_ROWS = slice(DH, 2 * DH)
V_ROWS = slice(0, DH)


def forward_kernel(len_ref, qk_ref, v_ref, out_ref, k_nat):
    blocks = k_nat.shape[0]
    ends = user_edges(len_ref)
    natural(qk_ref, K_ROWS, k_nat)
    for row_block in range(blocks):
        q_t = lane_pair(qk_ref, row_block, Q_ROWS)
        positions, starts = block_rows(row_block, ends)

        def step(col_block, total, q_t=q_t, positions=positions, starts=starts, row_block=row_block):
            raw = jnp.dot(k_nat[col_block], q_t, preferred_element_type=F32)
            half = raw * (0.5 / math.sqrt(DH))
            gate = 0.5 * jnp.tanh(half) + 0.5
            silu = (half + half) * gate
            allowed = tile_allowed(row_block, col_block, starts, positions)
            attn = jnp.where(allowed, silu, 0.0).astype(BF16)
            return total + jnp.dot(
                lane_pair(v_ref, col_block, V_ROWS), attn, preferred_element_type=F32
            )

        total = lax.fori_loop(
            first_block(row_block, ends), row_block + 1, step, jnp.zeros((DH, TILE), F32)
        )
        total = total * user_inverse(positions, ends, len_ref)
        out_ref[2 * row_block] = total[:, :LANES].astype(BF16)
        out_ref[2 * row_block + 1] = total[:, LANES:].astype(BF16)


def backward_kernel(len_ref, qk_ref, v_ref, g_ref, out_ref, k_nat, v_nat, k_acc, v_acc):
    blocks = k_nat.shape[0]
    scale = 1.0 / math.sqrt(DH)
    ends = user_edges(len_ref)
    natural(qk_ref, K_ROWS, k_nat)
    natural(v_ref, V_ROWS, v_nat)
    k_acc[...] = jnp.zeros_like(k_acc)
    v_acc[...] = jnp.zeros_like(v_acc)
    contract_lanes = (((1,), (1,)), ((), ()))
    for row_block in range(blocks):
        q_t = lane_pair(qk_ref, row_block, Q_ROWS)
        g_t = lane_pair(g_ref, row_block, slice(0, DH))
        positions, starts = block_rows(row_block, ends)

        def step(
            col_block, total, q_t=q_t, g_t=g_t, positions=positions, starts=starts, row_block=row_block
        ):
            raw = jnp.dot(k_nat[col_block], q_t, preferred_element_type=F32)
            attn_grad = jnp.dot(v_nat[col_block], g_t, preferred_element_type=F32)
            half = raw * (0.5 * scale)
            gate = 0.5 * jnp.tanh(half) + 0.5
            silu = (half + half) * gate
            slope = gate + silu * (1.0 - gate)
            allowed = tile_allowed(row_block, col_block, starts, positions)
            attn = jnp.where(allowed, silu, 0.0).astype(BF16)
            score_grad = jnp.where(allowed, attn_grad * slope, 0.0).astype(BF16)
            v_acc[col_block] += lax.dot_general(
                g_t, attn, contract_lanes, preferred_element_type=F32
            )
            k_acc[col_block] += lax.dot_general(
                q_t, score_grad, contract_lanes, preferred_element_type=F32
            )
            return total + jnp.dot(
                lane_pair(qk_ref, col_block, K_ROWS), score_grad, preferred_element_type=F32
            )

        total = lax.fori_loop(
            first_block(row_block, ends), row_block + 1, step, jnp.zeros((DH, TILE), F32)
        )
        total = (total * scale).astype(BF16)
        out_ref[2 * row_block, 0:DH, :] = total[:, :LANES]
        out_ref[2 * row_block + 1, 0:DH, :] = total[:, LANES:]
    for block in range(blocks):
        k_grad = (k_acc[block] * scale).astype(BF16)
        v_grad = v_acc[block].astype(BF16)
        for half in range(2):
            lanes = slice(half * LANES, (half + 1) * LANES)
            out_ref[2 * block + half, DH : 2 * DH, :] = k_grad[:, lanes]
            out_ref[2 * block + half, 2 * DH : 3 * DH, :] = v_grad[:, lanes]


def norm_kernel(
    len_ref, place_ref, o_ref, w_ref, out_grad_ref, gate_ref, grad_ref, gated_ref, gate_grad_ref, proj_acc
):
    width = w_ref.shape[0]
    tokens = out_grad_ref.shape[0]
    block = 256
    contract_lanes = (((1,), (1,)), ((), ()))
    out_grad = out_grad_ref[...]
    attn = o_ref[...].reshape(width, tokens).astype(F32)
    mean = jnp.sum(attn, axis=0, keepdims=True) * (1.0 / width)
    centred = attn - mean
    var = jnp.sum(centred * centred, axis=0, keepdims=True) * (1.0 / width)
    rstd = lax.rsqrt(var + 1e-05)
    sum_first = jnp.zeros((1, tokens), F32)
    sum_second = jnp.zeros((1, tokens), F32)
    for i in range(width // block):
        rows = slice(i * block, (i + 1) * block)
        gated_grad = lax.dot_general(
            w_ref[rows, :], out_grad, contract_lanes, preferred_element_type=F32
        )
        normed = (o_ref[i * block // DH : (i + 1) * block // DH].reshape(block, tokens).astype(F32) - mean) * rstd
        gates = gate_ref[:, rows].T.astype(F32)
        gated_ref[rows, :] = (normed * gates).astype(BF16)
        gate_grad_ref[:, rows] = (gated_grad * normed).astype(BF16).T
        normed_grad = gated_grad * gates
        sum_first = sum_first + jnp.sum(normed_grad, axis=0, keepdims=True)
        sum_second = sum_second + jnp.sum(normed_grad * normed, axis=0, keepdims=True)
        proj_acc[rows, :] = normed_grad
    sum_first = sum_first * (1.0 / width)
    sum_second = sum_second * (1.0 / width)
    position = place_ref[0] * tokens + lax.broadcasted_iota(jnp.int32, (1, tokens), 1)
    weight = rstd * user_inverse(position, user_edges(len_ref), len_ref)
    for i in range(width // block):
        rows = slice(i * block, (i + 1) * block)
        normed = (o_ref[i * block // DH : (i + 1) * block // DH].reshape(block, tokens).astype(F32) - mean) * rstd
        grad = (proj_acc[rows, :] - sum_first - normed * sum_second) * weight
        grad_ref[i * block // DH : (i + 1) * block // DH] = grad.astype(BF16).reshape(
            block // DH, DH, tokens
        )


def proj_kernel(mine_ref, other_ref, out_grad_ref, other_grad_ref, out_ref):
    chips, rows, width = out_ref.shape
    tokens = out_grad_ref.shape[0]
    step = 8
    for i in range(chips // step):
        part = slice(i * step, (i + 1) * step)
        mine = mine_ref[part].reshape(step * rows, tokens)
        other = other_ref[part].reshape(step * rows, tokens)
        left = jnp.concatenate([mine, other], axis=1)
        for j in range(width // 256):
            cols = slice(j * 256, (j + 1) * 256)
            right = jnp.concatenate([out_grad_ref[:, cols], other_grad_ref[:, cols]], axis=0)
            product = jnp.dot(left, right, preferred_element_type=F32)
            out_ref[part, :, cols] = product.astype(BF16).reshape(step, rows, 256)


def sum_kernel(x_ref, out_ref):
    out_ref[...] = jnp.sum(x_ref[...].astype(F32), axis=0).astype(BF16)


def exchange(array, axis, groups=None):
    return lax.all_to_all(
        array, axis, split_axis=0, concat_axis=0, tiled=True, axis_index_groups=groups
    )


def local(query_rows, key_rows, value_rows, gate_rows, out_grad, proj_weight, user_lengths):
    ctx = lax.axis_size("ctx")
    dp = lax.axis_size("dp")
    tokens, width = query_rows.shape
    heads = width // DH
    group = tokens * ctx
    blocks = group // TILE
    w_rows = proj_weight.size // LANES
    shape = jax.ShapeDtypeStruct
    partner = [(i, i ^ 1) for i in range(dp)]
    same_core = [[2 * i + core for i in range(dp // 2)] for core in range(2)]

    other_grad = lax.ppermute(out_grad, "dp", partner)
    first, second = call(
        pack_kernel,
        [
            shape((heads, 2 * DH + w_rows, tokens), BF16),
            shape((heads, DH, tokens), BF16),
        ],
        [VMEM] * 4,
        nbytes=6 * tokens * width * 2,
    )(query_rows, key_rows, value_rows, proj_weight.reshape(w_rows, LANES))
    first = exchange(first, "ctx")
    weight_part = first[:, 2 * DH :, :].reshape(ctx * proj_weight.shape[0], width)
    weights = lax.all_gather(weight_part, "dp", axis=0, tiled=True)
    second, first = lax.optimization_barrier((second, first))
    second = exchange(second, "ctx")

    attn_out = call(
        forward_kernel,
        shape((ctx, DH, tokens), BF16),
        [SMEM, VMEM, VMEM],
        [pltpu.VMEM((blocks, TILE, DH), BF16)],
        flops=group * group * DH * 2,
        nbytes=5 * group * DH * 2,
    )(user_lengths, first, second)
    attn_out = exchange(attn_out, "ctx")

    place = lax.axis_index("ctx").astype(jnp.int32).reshape(1)
    grad, gated, gate_grad = call(
        norm_kernel,
        [
            shape((heads, DH, tokens), BF16),
            shape((width, tokens), BF16),
            shape((tokens, width), BF16),
        ],
        [SMEM, SMEM, VMEM, VMEM, VMEM, VMEM],
        [pltpu.VMEM((width, tokens), F32)],
        flops=2 * tokens * width * width,
        nbytes=2 * width * width + 12 * tokens * width,
    )(user_lengths, place, attn_out, weights, out_grad, gate_rows)
    grad_heads = exchange(grad, "ctx")

    core = lax.rem(lax.axis_index("dp"), 2)
    gated = gated.reshape(dp // 2, 2, width // dp, tokens)
    mine = lax.dynamic_index_in_dim(gated, core, 1, keepdims=False)
    other = lax.dynamic_index_in_dim(gated, 1 - core, 1, keepdims=False)
    other = lax.ppermute(other, "dp", partner)
    partial = call(
        proj_kernel,
        shape((dp // 2, width // dp, width), BF16),
        [VMEM] * 4,
        flops=2 * tokens * width * width,
        nbytes=2 * width * width,
    )(mine, other, out_grad, other_grad)
    partial = exchange(partial, "dp", same_core)

    grads = call(
        backward_kernel,
        shape((ctx, 3 * DH, tokens), BF16),
        [SMEM, VMEM, VMEM, VMEM],
        [
            pltpu.VMEM((blocks, TILE, DH), BF16),
            pltpu.VMEM((blocks, TILE, DH), BF16),
            pltpu.VMEM((blocks, DH, TILE), F32),
            pltpu.VMEM((blocks, DH, TILE), F32),
        ],
        flops=3 * group * group * DH * 2,
        nbytes=7 * group * DH * 2,
    )(user_lengths, first, second, grad_heads)
    own = call(sum_kernel, shape((width // dp, width), BF16), [VMEM], nbytes=width * width)(partial)
    own = own.reshape(ctx, w_rows, LANES)
    grads = exchange(jnp.concatenate([grads, own], axis=1), "ctx")
    summed = jnp.sum(grads[:, 3 * DH :, :].astype(F32), axis=0).astype(BF16)
    proj = exchange(jnp.broadcast_to(summed[None], (ctx, w_rows, LANES)), "ctx")
    proj_grad = proj.reshape(width // dp, width).astype(F32)

    query_grad, key_grad, value_grad = call(
        functools.partial(unpack_kernel, 3),
        [shape((tokens, width), BF16)] * 3,
        [VMEM],
        nbytes=6 * tokens * width * 2,
    )(grads)
    return (query_grad, key_grad, value_grad, gate_grad, proj_grad)


def solution(mesh):
    rows = P(("dp", "ctx"), None)
    in_specs = (rows,) * 6 + (P("dp", None),)
    out_specs = (rows,) * 4 + (P("dp", None),)
    return jax.shard_map(local, mesh=mesh, in_specs=in_specs, out_specs=out_specs, check_vma=False)
```

```python
import functools
import math

import jax
import jax.numpy as jnp
from jax import lax
from jax.experimental import pallas as pl
from jax.experimental.pallas import tpu as pltpu
from jax.sharding import PartitionSpec as P

DH = 64
LANES = 128
TILE = 256
BF16 = jnp.bfloat16
F32 = jnp.float32
VMEM = pl.BlockSpec(memory_space=pltpu.VMEM)
SMEM = pl.BlockSpec(memory_space=pltpu.SMEM)
LIMIT = 48 * 1024 * 1024


def call(kernel, out_shape, in_specs, scratch=(), flops=0, nbytes=0):
    single = not isinstance(out_shape, (list, tuple))
    out_specs = VMEM if single else [VMEM] * len(out_shape)
    return pl.pallas_call(
        kernel,
        out_shape=out_shape,
        in_specs=in_specs,
        out_specs=out_specs,
        scratch_shapes=list(scratch),
        compiler_params=pltpu.CompilerParams(vmem_limit_bytes=LIMIT),
        cost_estimate=pl.CostEstimate(flops=flops, bytes_accessed=nbytes, transcendentals=0),
    )


def pack_kernel(q_hbm, k_hbm, v_hbm, out_ref, rows_ref, sems):
    heads = out_ref.shape[0]
    copies = [
        pltpu.make_async_copy(source, rows_ref.at[i], sems.at[i])
        for i, source in enumerate((q_hbm, k_hbm, v_hbm))
    ]
    for copy in copies:
        copy.start()
    for i, copy in enumerate(copies):
        copy.wait()
        for pair in range(heads // 2):
            both = rows_ref[i, :, pair * 2 * DH : (pair + 1) * 2 * DH].T
            out_ref[2 * pair, i * DH : (i + 1) * DH, :] = both[:DH]
            out_ref[2 * pair + 1, i * DH : (i + 1) * DH, :] = both[DH:]


def unpack_kernel(count, x_ref, *out_refs):
    heads = x_ref.shape[0]
    for pair in range(heads // 2):
        for i in range(count):
            rows = slice(i * DH, (i + 1) * DH)
            both = jnp.concatenate([x_ref[2 * pair, rows, :], x_ref[2 * pair + 1, rows, :]], axis=0)
            out_refs[i][:, pair * 2 * DH : (pair + 1) * 2 * DH] = both.T


def user_edges(len_ref):
    ends = []
    total = 0
    for i in range(len_ref.shape[1]):
        total = total + len_ref[0, i]
        ends.append(total)
    return ends


def user_start(position, ends):
    start = jnp.zeros_like(position)
    for end in ends[:-1]:
        start = jnp.where(position >= end, end, start)
    return start


def user_inverse(position, ends, len_ref):
    length = jnp.full(position.shape, len_ref[0, 0], jnp.int32)
    for i, end in enumerate(ends[:-1]):
        length = jnp.where(position >= end, len_ref[0, i + 1], length)
    return 1.0 / length.astype(F32)


def lane_pair(ref, block, rows):
    return jnp.concatenate([ref[2 * block, rows, :], ref[2 * block + 1, rows, :]], axis=1)


def tile_allowed(diagonal, col_block, starts, positions):
    key_pos = lax.broadcasted_iota(jnp.int32, (TILE, TILE), 0)
    shift = col_block * TILE
    allowed = key_pos >= starts - shift
    return allowed & (key_pos <= positions - shift) if diagonal else allowed


def block_rows(row_block, ends):
    positions = row_block * TILE + lax.broadcasted_iota(jnp.int32, (1, TILE), 1)
    return positions, user_start(positions, ends)


def first_block(row_block, ends):
    return lax.div(user_start(row_block * TILE, ends), TILE)


def natural(source_ref, rows, target_ref):
    for block in range(target_ref.shape[0]):
        for half in range(2):
            target_ref[block, half * LANES : (half + 1) * LANES, :] = source_ref[
                2 * block + half, rows, :
            ].T


Q_ROWS = slice(0, DH)
K_ROWS = slice(DH, 2 * DH)
V_ROWS = slice(2 * DH, 3 * DH)
CONTRACT_LANES = (((1,), (1,)), ((), ()))


def gate_and_silu(raw):
    half = raw * (0.5 / math.sqrt(DH))
    gate = 0.5 * jnp.tanh(half) + 0.5
    return gate, (half + half) * gate


def forward_kernel(len_ref, qkv_ref, out_ref, k_nat, attn_ref):
    ends = user_edges(len_ref)
    natural(qkv_ref, K_ROWS, k_nat)
    for row_block in range(k_nat.shape[0]):
        q_t = lane_pair(qkv_ref, row_block, Q_ROWS)
        positions, starts = block_rows(row_block, ends)
        first = first_block(row_block, ends)

        def score(col, diagonal, q_t=q_t, positions=positions, starts=starts):
            raw = jnp.dot(k_nat[col], q_t, preferred_element_type=F32)
            _, silu = gate_and_silu(raw)
            allowed = tile_allowed(diagonal, col, starts, positions)
            return jnp.where(allowed, silu, 0.0).astype(BF16)

        def product(col, attn):
            return jnp.dot(lane_pair(qkv_ref, col, V_ROWS), attn, preferred_element_type=F32)

        def step(i, total, row_block=row_block, score=score):
            col = row_block - 1 - i
            before = attn_ref[...]
            attn = score(col, False)
            total = total + product(col + 1, before)
            attn_ref[...] = attn
            return total

        attn_ref[...] = score(row_block, True)
        total = lax.fori_loop(0, row_block - first, step, jnp.zeros((DH, TILE), F32))
        total = total + product(first, attn_ref[...])
        total = total * user_inverse(positions, ends, len_ref)
        out_ref[2 * row_block] = total[:, :LANES].astype(BF16)
        out_ref[2 * row_block + 1] = total[:, LANES:].astype(BF16)


def backward_kernel(len_ref, qkv_ref, g_ref, out_ref, k_nat, v_nat, k_acc, v_acc, attn_ref, slope_ref):
    blocks = k_nat.shape[0]
    scale = 1.0 / math.sqrt(DH)
    ends = user_edges(len_ref)
    natural(qkv_ref, K_ROWS, k_nat)
    natural(qkv_ref, V_ROWS, v_nat)
    k_acc[...] = jnp.zeros_like(k_acc)
    v_acc[...] = jnp.zeros_like(v_acc)
    for row_block in range(blocks):
        q_t = lane_pair(qkv_ref, row_block, Q_ROWS)
        g_t = lane_pair(g_ref, row_block, slice(0, DH))
        positions, starts = block_rows(row_block, ends)
        first = first_block(row_block, ends)

        def score(col, diagonal, q_t=q_t, g_t=g_t, positions=positions, starts=starts):
            raw = jnp.dot(k_nat[col], q_t, preferred_element_type=F32)
            attn_grad = jnp.dot(v_nat[col], g_t, preferred_element_type=F32)
            gate, silu = gate_and_silu(raw)
            score_grad = attn_grad * (gate + silu * (1.0 - gate))
            allowed = tile_allowed(diagonal, col, starts, positions)
            return (
                jnp.where(allowed, silu, 0.0).astype(BF16),
                jnp.where(allowed, score_grad, 0.0).astype(BF16),
            )

        def product(col, attn, score_grad, q_t=q_t, g_t=g_t):
            v_acc[col] += lax.dot_general(g_t, attn, CONTRACT_LANES, preferred_element_type=F32)
            k_acc[col] += lax.dot_general(
                q_t, score_grad, CONTRACT_LANES, preferred_element_type=F32
            )
            return jnp.dot(lane_pair(qkv_ref, col, K_ROWS), score_grad, preferred_element_type=F32)

        def step(i, total, row_block=row_block, score=score, product=product):
            col = row_block - 1 - i
            before = attn_ref[...], slope_ref[...]
            attn, score_grad = score(col, False)
            total = total + product(col + 1, *before)
            attn_ref[...] = attn
            slope_ref[...] = score_grad
            return total

        attn, score_grad = score(row_block, True)
        attn_ref[...] = attn
        slope_ref[...] = score_grad
        total = lax.fori_loop(0, row_block - first, step, jnp.zeros((DH, TILE), F32))
        total = total + product(first, attn_ref[...], slope_ref[...])
        total = (total * scale).astype(BF16)
        out_ref[2 * row_block, 0:DH, :] = total[:, :LANES]
        out_ref[2 * row_block + 1, 0:DH, :] = total[:, LANES:]
    for block in range(blocks):
        k_grad = (k_acc[block] * scale).astype(BF16)
        v_grad = v_acc[block].astype(BF16)
        for half in range(2):
            lanes = slice(half * LANES, (half + 1) * LANES)
            out_ref[2 * block + half, DH : 2 * DH, :] = k_grad[:, lanes]
            out_ref[2 * block + half, 2 * DH : 3 * DH, :] = v_grad[:, lanes]


def project_kernel(
    place_ref, w0_ref, w1_ref, w2_low_ref, w2_high_ref, w3_ref, out_grad_ref, other_grad_ref, mine_ref, theirs_ref
):
    side, rows, width = w0_ref.shape
    tokens = out_grad_ref.shape[0]
    both = jnp.concatenate([out_grad_ref[...], other_grad_ref[...]], axis=0)
    pieces = [(w0_ref, 0, 0), (w1_ref, 1, 0), (w2_low_ref, 2, 0), (w2_high_ref, 2, side // 2), (w3_ref, 3, 0)]
    for ref, y_back, x_first in pieces:
        count = ref.shape[0]
        product = lax.dot_general(
            ref[...].reshape(count * rows, width), both, CONTRACT_LANES, preferred_element_type=F32
        )
        y = lax.rem(place_ref[3] + side - y_back, side)
        for i in range(count):
            x = lax.rem(place_ref[2] + side - x_first - i, side)
            mine_ref[x * side + y] = product[i * rows : (i + 1) * rows, :tokens]
            theirs_ref[x * side + y] = product[i * rows : (i + 1) * rows, tokens:]


def norm_kernel(
    len_ref,
    place_ref,
    o_ref,
    mine_ref,
    recv_ref,
    gate_ref,
    grad_ref,
    gated_mine_ref,
    gated_other_ref,
    gate_grad_ref,
    normed_grad_ref,
):
    heads, _, tokens = o_ref.shape
    width = heads * DH
    half = DH // 2
    even = place_ref[1] == 0
    total = jnp.zeros((DH, tokens), F32)
    for head in range(heads):
        total = total + o_ref[head].astype(F32)
    mean = jnp.sum(total, axis=0, keepdims=True) * (1.0 / width)
    total = jnp.zeros((DH, tokens), F32)
    for head in range(heads):
        centred = o_ref[head].astype(F32) - mean
        total = total + centred * centred
    var = jnp.sum(total, axis=0, keepdims=True) * (1.0 / width)
    rstd = lax.rsqrt(var + 1e-05)
    first = jnp.zeros((DH, tokens), F32)
    second = jnp.zeros((DH, tokens), F32)
    for pair in range(heads // 2):
        cols = slice(pair * 2 * DH, (pair + 1) * 2 * DH)
        gates = gate_ref[:, cols].T.astype(F32)
        gate_grads = []
        for i in range(2):
            head = 2 * pair + i
            normed = (o_ref[head].astype(F32) - mean) * rstd
            mine, recv = mine_ref[head], recv_ref[head]
            gated_grad = jnp.concatenate(
                [jnp.where(even, mine, recv), jnp.where(even, recv, mine)], axis=0
            )
            gate = gates[i * DH : (i + 1) * DH]
            gated = normed * gate
            low, high = gated[:half], gated[half:]
            gated_mine_ref[head] = jnp.where(even, low, high).astype(BF16)
            gated_other_ref[head] = jnp.where(even, high, low).astype(BF16)
            gate_grads.append((gated_grad * normed).astype(BF16))
            normed_grad = gated_grad * gate
            first = first + normed_grad
            second = second + normed_grad * normed
            normed_grad_ref[head] = normed_grad
        gate_grad_ref[:, cols] = jnp.concatenate(gate_grads, axis=0).T
    first = jnp.sum(first, axis=0, keepdims=True) * (1.0 / width)
    second = jnp.sum(second, axis=0, keepdims=True) * (1.0 / width)
    position = place_ref[0] * tokens + lax.broadcasted_iota(jnp.int32, (1, tokens), 1)
    weight = rstd * user_inverse(position, user_edges(len_ref), len_ref)
    for head in range(heads):
        normed = (o_ref[head].astype(F32) - mean) * rstd
        grad_ref[head] = ((normed_grad_ref[head] - first - normed * second) * weight).astype(BF16)


def proj_kernel(mine_ref, other_ref, out_grad_ref, other_grad_ref, out_ref):
    chips, rows, width = out_ref.shape
    tokens = out_grad_ref.shape[0]
    step = 8
    for i in range(chips // step):
        part = slice(i * step, (i + 1) * step)
        mine = mine_ref[part].reshape(step * rows, tokens)
        other = other_ref[part].reshape(step * rows, tokens)
        left = jnp.concatenate([mine, other], axis=1)
        for j in range(width // 256):
            cols = slice(j * 256, (j + 1) * 256)
            right = jnp.concatenate([out_grad_ref[:, cols], other_grad_ref[:, cols]], axis=0)
            product = jnp.dot(left, right, preferred_element_type=F32)
            out_ref[part, :, cols] = product.astype(BF16).reshape(step, rows, 256)


def sum_kernel(x_ref, out_ref):
    out_ref[...] = jnp.sum(x_ref[...].astype(F32), axis=0).astype(BF16)


def exchange(array, axis, groups=None):
    return lax.all_to_all(
        array, axis, split_axis=0, concat_axis=0, tiled=True, axis_index_groups=groups
    )


SIDE = 4


def plane_shift(axis, step):
    moves = []
    for i in range(2 * SIDE * SIDE):
        x, y, core = i // (2 * SIDE), i // 2 % SIDE, i % 2
        if axis == "x":
            x = (x + step) % SIDE
        else:
            y = (y + step) % SIDE
        moves.append((i, (x * SIDE + y) * 2 + core))
    return moves


def ring_blocks(block, axis):
    up, down = plane_shift(axis, 1), plane_shift(axis, -1)
    back_one = lax.ppermute(block, "dp", up)
    back_three = lax.ppermute(block, "dp", down)
    half = block.shape[0] // 2
    low = lax.ppermute(back_one[:half], "dp", up)
    high = lax.ppermute(back_three[half:], "dp", down)
    return block, back_one, low, high, back_three


def local(query_rows, key_rows, value_rows, gate_rows, out_grad, proj_weight, user_lengths):
    ctx = lax.axis_size("ctx")
    dp = lax.axis_size("dp")
    tokens, width = query_rows.shape
    heads = width // DH
    group = tokens * ctx
    blocks = group // TILE
    chips = dp // 2
    out_rows = width // dp
    w_rows = proj_weight.size // LANES
    shape = jax.ShapeDtypeStruct
    partner = [(i, i ^ 1) for i in range(dp)]
    same_core = [[2 * i + core for i in range(chips)] for core in range(2)]
    chip = lax.axis_index("dp") // 2
    place = jnp.stack(
        [lax.axis_index("ctx"), lax.rem(lax.axis_index("dp"), 2), chip // SIDE, lax.rem(chip, SIDE)]
    ).astype(jnp.int32)
    in_hbm = pl.BlockSpec(memory_space=pltpu.HBM)

    block = proj_weight.reshape(1, w_rows, LANES)
    block = exchange(jnp.broadcast_to(block, (ctx, w_rows, LANES)), "ctx")
    qkv = call(
        pack_kernel,
        shape((heads, 3 * DH, tokens), BF16),
        [in_hbm] * 3,
        [pltpu.VMEM((3, tokens, width), BF16), pltpu.SemaphoreType.DMA((3,))],
        nbytes=6 * tokens * width * 2,
    )(query_rows, key_rows, value_rows)
    block, qkv = lax.optimization_barrier((block, qkv))
    qkv = exchange(qkv, "ctx")

    block = block.reshape(out_rows, width)
    column = jnp.concatenate(ring_blocks(block, "x"), axis=0).reshape(SIDE, out_rows, width)
    weights = ring_blocks(column, "y")
    qkv, weights = lax.optimization_barrier((qkv, weights))
    other_grad = lax.ppermute(out_grad, "dp", partner)
    mine, theirs = call(
        project_kernel,
        [shape((heads, DH // 2, tokens), F32)] * 2,
        [SMEM] + [VMEM] * 7,
        flops=2 * tokens * width * width,
        nbytes=2 * width * width,
    )(place, *weights, out_grad, other_grad)
    received = lax.ppermute(theirs, "dp", partner)

    attn_out = call(
        forward_kernel,
        shape((ctx, DH, tokens), BF16),
        [SMEM, VMEM],
        [pltpu.VMEM((blocks, TILE, DH), BF16), pltpu.VMEM((TILE, TILE), BF16)],
        flops=group * group * DH * 2,
        nbytes=5 * group * DH * 2,
    )(user_lengths, qkv)
    attn_out = exchange(attn_out, "ctx")

    grad, gated_mine, gated_other, gate_grad = call(
        norm_kernel,
        [
            shape((heads, DH, tokens), BF16),
            shape((heads, DH // 2, tokens), BF16),
            shape((heads, DH // 2, tokens), BF16),
            shape((tokens, width), BF16),
        ],
        [SMEM, SMEM, VMEM, VMEM, VMEM, VMEM],
        [pltpu.VMEM((heads, DH, tokens), F32)],
        nbytes=18 * tokens * width,
    )(user_lengths, place, attn_out, mine, received, gate_rows)
    grad = exchange(grad, "ctx")

    other = lax.ppermute(gated_other, "dp", partner)
    partial = call(
        proj_kernel,
        shape((chips, out_rows, width), BF16),
        [VMEM] * 4,
        flops=2 * tokens * width * width,
        nbytes=2 * width * width,
    )(gated_mine, other, out_grad, other_grad)
    partial = exchange(partial, "dp", same_core)

    grads = call(
        backward_kernel,
        shape((ctx, 3 * DH, tokens), BF16),
        [SMEM, VMEM, VMEM],
        [
            pltpu.VMEM((blocks, TILE, DH), BF16),
            pltpu.VMEM((blocks, TILE, DH), BF16),
            pltpu.VMEM((blocks, DH, TILE), F32),
            pltpu.VMEM((blocks, DH, TILE), F32),
            pltpu.VMEM((TILE, TILE), BF16),
            pltpu.VMEM((TILE, TILE), BF16),
        ],
        flops=3 * group * group * DH * 2,
        nbytes=7 * group * DH * 2,
    )(user_lengths, qkv, grad)
    own = call(sum_kernel, shape((out_rows, width), BF16), [VMEM], nbytes=width * width)(partial)
    own = own.reshape(ctx, w_rows, LANES)
    grads = exchange(jnp.concatenate([grads, own], axis=1), "ctx")
    summed = jnp.sum(grads[:, 3 * DH :, :].astype(F32), axis=0).astype(BF16)
    proj = exchange(jnp.broadcast_to(summed[None], (ctx, w_rows, LANES)), "ctx")
    proj_grad = proj.reshape(out_rows, width).astype(F32)

    query_grad, key_grad, value_grad = call(
        functools.partial(unpack_kernel, 3),
        [shape((tokens, width), BF16)] * 3,
        [VMEM],
        nbytes=6 * tokens * width * 2,
    )(grads)
    return (query_grad, key_grad, value_grad, gate_grad, proj_grad)


def solution(mesh):
    rows = P(("dp", "ctx"), None)
    in_specs = (rows,) * 6 + (P("dp", None),)
    out_specs = (rows,) * 4 + (P("dp", None),)
    return jax.shard_map(local, mesh=mesh, in_specs=in_specs, out_specs=out_specs, check_vma=False)
```

```python
import math

import jax
import jax.numpy as jnp
from jax import lax
from jax.experimental import pallas as pl
from jax.experimental.pallas import tpu as pltpu
from jax.sharding import PartitionSpec as P

DH = 64
LANES = 128
TILE = 256
SUM_ROWS = 16
BF16 = jnp.bfloat16
F32 = jnp.float32
VMEM = pl.BlockSpec(memory_space=pltpu.VMEM)
SMEM = pl.BlockSpec(memory_space=pltpu.SMEM)
LIMIT = 16 * 1024 * 1024


def call(kernel, out_shape, in_specs, scratch=(), flops=0, nbytes=0):
    single = not isinstance(out_shape, (list, tuple))
    out_specs = VMEM if single else [VMEM] * len(out_shape)
    return pl.pallas_call(
        kernel,
        out_shape=out_shape,
        in_specs=in_specs,
        out_specs=out_specs,
        scratch_shapes=list(scratch),
        compiler_params=pltpu.CompilerParams(vmem_limit_bytes=LIMIT),
        cost_estimate=pl.CostEstimate(flops=flops, bytes_accessed=nbytes, transcendentals=0),
    )


def spread_kernel(w_ref, out_ref):
    count, width = w_ref.shape
    weight = w_ref[...].astype(F32)
    pieces = [weight[:, j * LANES : (j + 1) * LANES] for j in range(width // LANES)]
    rows = jnp.concatenate(pieces, axis=0).astype(BF16)
    for chunk in range(out_ref.shape[0]):
        out_ref[chunk] = rows


def pack_kernel(q_hbm, k_hbm, v_hbm, out_ref, rows_ref, sems):
    heads = out_ref.shape[0]
    copies = [
        pltpu.make_async_copy(source, rows_ref.at[i], sems.at[i])
        for i, source in enumerate((q_hbm, k_hbm, v_hbm))
    ]
    for copy in copies:
        copy.start()
    for i, copy in enumerate(copies):
        copy.wait()
        for pair in range(heads // 2):
            both = rows_ref[i, :, pair * 2 * DH : (pair + 1) * 2 * DH].T
            out_ref[2 * pair, i * DH : (i + 1) * DH, :] = both[:DH]
            out_ref[2 * pair + 1, i * DH : (i + 1) * DH, :] = both[DH:]


def unpack_kernel(x_ref, q_ref, k_ref, v_ref, proj_ref):
    for pair in range(x_ref.shape[0] // 2):
        for i, out_ref in enumerate((q_ref, k_ref, v_ref)):
            rows = slice(i * DH, (i + 1) * DH)
            both = jnp.concatenate([x_ref[2 * pair, rows, :], x_ref[2 * pair + 1, rows, :]], axis=0)
            out_ref[:, pair * 2 * DH : (pair + 1) * 2 * DH] = both.T
    for row, col, chunk in proj_tiles(proj_ref.shape):
        proj_ref[row, col] = x_ref[chunk, 3 * DH :, :].astype(F32)


def proj_tiles(shape):
    rows, width = shape
    per_row = width // LANES
    for i in range(rows // SUM_ROWS):
        for j in range(per_row):
            yield (
                slice(i * SUM_ROWS, (i + 1) * SUM_ROWS),
                slice(j * LANES, (j + 1) * LANES),
                i * per_row + j,
            )


def user_edges(len_ref):
    ends = []
    total = 0
    for i in range(len_ref.shape[1]):
        total = total + len_ref[0, i]
        ends.append(total)
    return ends


def user_start(position, ends):
    start = jnp.zeros_like(position)
    for end in ends[:-1]:
        start = jnp.where(position >= end, end, start)
    return start


def user_inverse(position, ends, len_ref):
    length = jnp.full(position.shape, len_ref[0, 0], jnp.int32)
    for i, end in enumerate(ends[:-1]):
        length = jnp.where(position >= end, len_ref[0, i + 1], length)
    return 1.0 / length.astype(F32)


def lane_pair(ref, block, rows):
    return jnp.concatenate([ref[2 * block, rows, :], ref[2 * block + 1, rows, :]], axis=1)


def tile_allowed(diagonal, col_block, starts, positions):
    key_pos = lax.broadcasted_iota(jnp.int32, (TILE, TILE), 0)
    shift = col_block * TILE
    allowed = key_pos >= starts - shift
    return allowed & (key_pos <= positions - shift) if diagonal else allowed


def block_rows(row_block, ends):
    positions = row_block * TILE + lax.broadcasted_iota(jnp.int32, (1, TILE), 1)
    return positions, user_start(positions, ends)


def first_block(row_block, ends):
    return lax.div(user_start(row_block * TILE, ends), TILE)


def natural(source_ref, rows, target_ref):
    for block in range(target_ref.shape[0]):
        for half in range(2):
            target_ref[block, half * LANES : (half + 1) * LANES, :] = source_ref[
                2 * block + half, rows, :
            ].T


Q_ROWS = slice(0, DH)
K_ROWS = slice(DH, 2 * DH)
V_ROWS = slice(2 * DH, 3 * DH)
CONTRACT_LANES = (((1,), (1,)), ((), ()))


def gate_and_silu(raw):
    half = raw * (0.5 / math.sqrt(DH))
    gate = 0.5 * jnp.tanh(half) + 0.5
    return gate, (half + half) * gate


def forward_kernel(len_ref, qkv_ref, out_ref, k_nat, attn_ref):
    ends = user_edges(len_ref)
    natural(qkv_ref, K_ROWS, k_nat)
    for row_block in range(k_nat.shape[0]):
        q_t = lane_pair(qkv_ref, row_block, Q_ROWS)
        positions, starts = block_rows(row_block, ends)
        first = first_block(row_block, ends)

        def score(col, diagonal, q_t=q_t, positions=positions, starts=starts):
            raw = jnp.dot(k_nat[col], q_t, preferred_element_type=F32)
            _, silu = gate_and_silu(raw)
            allowed = tile_allowed(diagonal, col, starts, positions)
            return jnp.where(allowed, silu, 0.0).astype(BF16)

        def product(col, attn):
            return jnp.dot(lane_pair(qkv_ref, col, V_ROWS), attn, preferred_element_type=F32)

        def step(i, total, row_block=row_block, score=score):
            col = row_block - 1 - i
            before = attn_ref[...]
            attn = score(col, False)
            total = total + product(col + 1, before)
            attn_ref[...] = attn
            return total

        attn_ref[...] = score(row_block, True)
        total = lax.fori_loop(0, row_block - first, step, jnp.zeros((DH, TILE), F32))
        total = total + product(first, attn_ref[...])
        total = total * user_inverse(positions, ends, len_ref)
        out_ref[2 * row_block] = total[:, :LANES].astype(BF16)
        out_ref[2 * row_block + 1] = total[:, LANES:].astype(BF16)


def backward_kernel(len_ref, qkv_ref, g_ref, out_ref, k_nat, v_nat, k_acc, v_acc, attn_ref, slope_ref):
    blocks = k_nat.shape[0]
    scale = 1.0 / math.sqrt(DH)
    ends = user_edges(len_ref)
    natural(qkv_ref, K_ROWS, k_nat)
    natural(qkv_ref, V_ROWS, v_nat)
    k_acc[...] = jnp.zeros_like(k_acc)
    v_acc[...] = jnp.zeros_like(v_acc)
    for row_block in range(blocks):
        q_t = lane_pair(qkv_ref, row_block, Q_ROWS)
        g_t = lane_pair(g_ref, row_block, slice(0, DH))
        positions, starts = block_rows(row_block, ends)
        first = first_block(row_block, ends)

        def score(col, diagonal, q_t=q_t, g_t=g_t, positions=positions, starts=starts):
            raw = jnp.dot(k_nat[col], q_t, preferred_element_type=F32)
            attn_grad = jnp.dot(v_nat[col], g_t, preferred_element_type=F32)
            gate, silu = gate_and_silu(raw)
            score_grad = attn_grad * (gate + silu * (1.0 - gate))
            allowed = tile_allowed(diagonal, col, starts, positions)
            return (
                jnp.where(allowed, silu, 0.0).astype(BF16),
                jnp.where(allowed, score_grad, 0.0).astype(BF16),
            )

        def product(col, attn, score_grad, q_t=q_t, g_t=g_t):
            v_acc[col] += lax.dot_general(g_t, attn, CONTRACT_LANES, preferred_element_type=F32)
            k_acc[col] += lax.dot_general(
                q_t, score_grad, CONTRACT_LANES, preferred_element_type=F32
            )
            return jnp.dot(lane_pair(qkv_ref, col, K_ROWS), score_grad, preferred_element_type=F32)

        def step(i, total, row_block=row_block, score=score, product=product):
            col = row_block - 1 - i
            before = attn_ref[...], slope_ref[...]
            attn, score_grad = score(col, False)
            total = total + product(col + 1, *before)
            attn_ref[...] = attn
            slope_ref[...] = score_grad
            return total

        attn, score_grad = score(row_block, True)
        attn_ref[...] = attn
        slope_ref[...] = score_grad
        total = lax.fori_loop(0, row_block - first, step, jnp.zeros((DH, TILE), F32))
        total = total + product(first, attn_ref[...], slope_ref[...])
        total = (total * scale).astype(BF16)
        out_ref[2 * row_block, 0:DH, :] = total[:, :LANES]
        out_ref[2 * row_block + 1, 0:DH, :] = total[:, LANES:]
    total = jnp.sum(g_ref[:, DH:, :].astype(F32), axis=0).astype(BF16)
    for chunk in range(out_ref.shape[0]):
        out_ref[chunk, 3 * DH :, :] = total
    for block in range(blocks):
        k_grad = (k_acc[block] * scale).astype(BF16)
        v_grad = v_acc[block].astype(BF16)
        for half in range(2):
            lanes = slice(half * LANES, (half + 1) * LANES)
            out_ref[2 * block + half, DH : 2 * DH, :] = k_grad[:, lanes]
            out_ref[2 * block + half, 2 * DH : 3 * DH, :] = v_grad[:, lanes]


def project_kernel(
    place_ref, w0_ref, w1_ref, w2_low_ref, w2_high_ref, w3_ref, out_grad_ref, other_grad_ref, mine_ref, theirs_ref
):
    side, rows, width = w0_ref.shape
    tokens = out_grad_ref.shape[0]
    both = jnp.concatenate([out_grad_ref[...], other_grad_ref[...]], axis=0)
    pieces = [(w0_ref, 0, 0), (w1_ref, 1, 0), (w2_low_ref, 2, 0), (w2_high_ref, 2, side // 2), (w3_ref, 3, 0)]
    for ref, y_back, x_first in pieces:
        count = ref.shape[0]
        product = lax.dot_general(
            ref[...].reshape(count * rows, width), both, CONTRACT_LANES, preferred_element_type=F32
        )
        y = lax.rem(place_ref[3] + side - y_back, side)
        for i in range(count):
            x = lax.rem(place_ref[2] + side - x_first - i, side)
            mine_ref[x * side + y] = product[i * rows : (i + 1) * rows, :tokens]
            theirs_ref[x * side + y] = product[i * rows : (i + 1) * rows, tokens:]


def norm_stats(o_ref):
    heads, _, tokens = o_ref.shape
    share = 1.0 / (heads * DH)
    total = jnp.zeros((DH, tokens), F32)
    for head in range(heads):
        total = total + o_ref[head].astype(F32)
    mean = jnp.sum(total, axis=0, keepdims=True) * share
    total = jnp.zeros((DH, tokens), F32)
    for head in range(heads):
        centred = o_ref[head].astype(F32) - mean
        total = total + centred * centred
    var = jnp.sum(total, axis=0, keepdims=True) * share
    return mean, lax.rsqrt(var + 1e-05)


def gated_kernel(place_ref, o_ref, gate_ref, mine_ref, other_ref):
    half = DH // 2
    even = place_ref[1] == 0
    mean, rstd = norm_stats(o_ref)
    for pair in range(o_ref.shape[0] // 2):
        gates = gate_ref[:, pair * 2 * DH : (pair + 1) * 2 * DH].T.astype(F32)
        for i in range(2):
            head = 2 * pair + i
            normed = (o_ref[head].astype(F32) - mean) * rstd
            gated = normed * gates[i * DH : (i + 1) * DH]
            low, high = gated[:half], gated[half:]
            mine_ref[head] = jnp.where(even, low, high).astype(BF16)
            other_ref[head] = jnp.where(even, high, low).astype(BF16)


def norm_kernel(
    len_ref, place_ref, o_ref, mine_ref, recv_ref, gate_ref, grad_ref, gate_grad_ref, normed_grad_ref
):
    heads, _, tokens = o_ref.shape
    width = heads * DH
    even = place_ref[1] == 0
    mean, rstd = norm_stats(o_ref)
    first = jnp.zeros((DH, tokens), F32)
    second = jnp.zeros((DH, tokens), F32)
    for pair in range(heads // 2):
        cols = slice(pair * 2 * DH, (pair + 1) * 2 * DH)
        gates = gate_ref[:, cols].T.astype(F32)
        gate_grads = []
        for i in range(2):
            head = 2 * pair + i
            normed = (o_ref[head].astype(F32) - mean) * rstd
            mine, recv = mine_ref[head], recv_ref[head]
            gated_grad = jnp.concatenate(
                [jnp.where(even, mine, recv), jnp.where(even, recv, mine)], axis=0
            )
            gate_grads.append((gated_grad * normed).astype(BF16))
            normed_grad = gated_grad * gates[i * DH : (i + 1) * DH]
            first = first + normed_grad
            second = second + normed_grad * normed
            normed_grad_ref[head] = normed_grad
        gate_grad_ref[:, cols] = jnp.concatenate(gate_grads, axis=0).T
    first = jnp.sum(first, axis=0, keepdims=True) * (1.0 / width)
    second = jnp.sum(second, axis=0, keepdims=True) * (1.0 / width)
    position = place_ref[0] * tokens + lax.broadcasted_iota(jnp.int32, (1, tokens), 1)
    weight = rstd * user_inverse(position, user_edges(len_ref), len_ref)
    for head in range(heads):
        normed = (o_ref[head].astype(F32) - mean) * rstd
        grad_ref[head] = ((normed_grad_ref[head] - first - normed * second) * weight).astype(BF16)


def proj_kernel(mine_ref, other_ref, out_grad_ref, other_grad_ref, out_ref):
    chips, rows, width = out_ref.shape
    tokens = out_grad_ref.shape[0]
    step = 8
    for i in range(chips // step):
        part = slice(i * step, (i + 1) * step)
        mine = mine_ref[part].reshape(step * rows, tokens)
        other = other_ref[part].reshape(step * rows, tokens)
        left = jnp.concatenate([mine, other], axis=1)
        for j in range(width // 256):
            cols = slice(j * 256, (j + 1) * 256)
            right = jnp.concatenate([out_grad_ref[:, cols], other_grad_ref[:, cols]], axis=0)
            product = jnp.dot(left, right, preferred_element_type=F32)
            out_ref[part, :, cols] = product.astype(BF16).reshape(step, rows, 256)


def sum_kernel(x_ref, grad_ref, out_ref):
    _, rows, width = x_ref.shape
    out_ref[:, :DH, :] = grad_ref[...]
    for row, col, chunk in proj_tiles((rows, width)):
        tile = jnp.sum(x_ref[:, row, col].astype(F32), axis=0)
        out_ref[chunk, DH:, :] = tile.astype(BF16)


def exchange(array, axis, groups=None):
    return lax.all_to_all(
        array, axis, split_axis=0, concat_axis=0, tiled=True, axis_index_groups=groups
    )


SIDE = 4


def plane_shift(axis, step):
    moves = []
    for i in range(2 * SIDE * SIDE):
        x, y, core = i // (2 * SIDE), i // 2 % SIDE, i % 2
        if axis == "x":
            x = (x + step) % SIDE
        else:
            y = (y + step) % SIDE
        moves.append((i, (x * SIDE + y) * 2 + core))
    return moves


def ring_blocks(block, axis):
    up, down = plane_shift(axis, 1), plane_shift(axis, -1)
    back_one = lax.ppermute(block, "dp", up)
    back_three = lax.ppermute(block, "dp", down)
    half = block.shape[0] // 2
    low = lax.ppermute(back_one[:half], "dp", up)
    high = lax.ppermute(back_three[half:], "dp", down)
    return block, back_one, low, high, back_three


def local(query_rows, key_rows, value_rows, gate_rows, out_grad, proj_weight, user_lengths):
    ctx = lax.axis_size("ctx")
    dp = lax.axis_size("dp")
    tokens, width = query_rows.shape
    heads = width // DH
    group = tokens * ctx
    blocks = group // TILE
    chips = dp // 2
    out_rows = width // dp
    w_rows = proj_weight.size // LANES
    shape = jax.ShapeDtypeStruct
    partner = [(i, i ^ 1) for i in range(dp)]
    same_core = [[2 * i + core for i in range(chips)] for core in range(2)]
    chip = lax.axis_index("dp") // 2
    place = jnp.stack(
        [lax.axis_index("ctx"), lax.rem(lax.axis_index("dp"), 2), chip // SIDE, lax.rem(chip, SIDE)]
    ).astype(jnp.int32)
    in_hbm = pl.BlockSpec(memory_space=pltpu.HBM)

    block = call(
        spread_kernel, shape((ctx, w_rows, LANES), BF16), [VMEM], nbytes=tokens * width
    )(proj_weight)
    block = exchange(block, "ctx")
    qkv = call(
        pack_kernel,
        shape((heads, 3 * DH, tokens), BF16),
        [in_hbm] * 3,
        [pltpu.VMEM((3, tokens, width), BF16), pltpu.SemaphoreType.DMA((3,))],
        nbytes=6 * tokens * width * 2,
    )(query_rows, key_rows, value_rows)
    block, qkv = lax.optimization_barrier((block, qkv))
    qkv = exchange(qkv, "ctx")

    block = block.reshape(ctx, width // LANES, out_rows // ctx, LANES).transpose(0, 2, 1, 3)
    block = block.reshape(out_rows, width)
    column = jnp.concatenate(ring_blocks(block, "x"), axis=0).reshape(SIDE, out_rows, width)
    weights = ring_blocks(column, "y")
    qkv, weights = lax.optimization_barrier((qkv, weights))
    other_grad = lax.ppermute(out_grad, "dp", partner)
    mine, theirs = call(
        project_kernel,
        [shape((heads, DH // 2, tokens), F32)] * 2,
        [SMEM] + [VMEM] * 7,
        flops=2 * tokens * width * width,
        nbytes=2 * width * width,
    )(place, *weights, out_grad, other_grad)
    received = lax.ppermute(theirs, "dp", partner)

    attn_out = call(
        forward_kernel,
        shape((ctx, DH, tokens), BF16),
        [SMEM, VMEM],
        [pltpu.VMEM((blocks, TILE, DH), BF16), pltpu.VMEM((TILE, TILE), BF16)],
        flops=group * group * DH * 2,
        nbytes=5 * group * DH * 2,
    )(user_lengths, qkv)
    attn_out = exchange(attn_out, "ctx")

    gated_mine, gated_other = call(
        gated_kernel,
        [shape((heads, DH // 2, tokens), BF16)] * 2,
        [SMEM, VMEM, VMEM],
        nbytes=6 * tokens * width,
    )(place, attn_out, gate_rows)
    other = lax.ppermute(gated_other, "dp", partner)
    partial = call(
        proj_kernel,
        shape((chips, out_rows, width), BF16),
        [VMEM] * 4,
        flops=2 * tokens * width * width,
        nbytes=2 * width * width,
    )(gated_mine, other, out_grad, other_grad)
    partial = exchange(partial, "dp", same_core)
    grad, gate_grad = call(
        norm_kernel,
        [shape((heads, DH, tokens), BF16), shape((tokens, width), BF16)],
        [SMEM, SMEM, VMEM, VMEM, VMEM, VMEM],
        [pltpu.VMEM((heads, DH, tokens), F32)],
        nbytes=18 * tokens * width,
    )(user_lengths, place, attn_out, mine, received, gate_rows)
    grad = call(
        sum_kernel,
        shape((ctx, DH + w_rows, tokens), BF16),
        [VMEM, VMEM],
        nbytes=width * width + 4 * tokens * width,
    )(partial, grad)
    grad = exchange(grad, "ctx")

    grads = call(
        backward_kernel,
        shape((ctx, 3 * DH + w_rows, tokens), BF16),
        [SMEM, VMEM, VMEM],
        [
            pltpu.VMEM((blocks, TILE, DH), BF16),
            pltpu.VMEM((blocks, TILE, DH), BF16),
            pltpu.VMEM((blocks, DH, TILE), F32),
            pltpu.VMEM((blocks, DH, TILE), F32),
            pltpu.VMEM((TILE, TILE), BF16),
            pltpu.VMEM((TILE, TILE), BF16),
        ],
        flops=3 * group * group * DH * 2,
        nbytes=7 * group * DH * 2,
    )(user_lengths, qkv, grad)
    grads = exchange(grads, "ctx")
    query_grad, key_grad, value_grad, proj_grad = call(
        unpack_kernel,
        [shape((tokens, width), BF16)] * 3 + [shape((out_rows, width), F32)],
        [VMEM],
        nbytes=6 * tokens * width * 2,
    )(grads)
    return (query_grad, key_grad, value_grad, gate_grad, proj_grad)


def solution(mesh):
    rows = P(("dp", "ctx"), None)
    in_specs = (rows,) * 6 + (P("dp", None),)
    out_specs = (rows,) * 4 + (P("dp", None),)
    return jax.shard_map(local, mesh=mesh, in_specs=in_specs, out_specs=out_specs, check_vma=False)
```

```python
import math

import jax
import jax.numpy as jnp
from jax import lax
from jax.experimental import pallas as pl
from jax.experimental.pallas import tpu as pltpu
from jax.sharding import PartitionSpec as P

DH = 64
LANES = 128
TILE = 256
SUM_ROWS = 16
BF16 = jnp.bfloat16
F32 = jnp.float32
VMEM = pl.BlockSpec(memory_space=pltpu.VMEM)
SMEM = pl.BlockSpec(memory_space=pltpu.SMEM)
LIMIT = 16 * 1024 * 1024


def call(kernel, out_shape, in_specs, scratch=(), flops=0, nbytes=0):
    single = not isinstance(out_shape, (list, tuple))
    out_specs = VMEM if single else [VMEM] * len(out_shape)
    return pl.pallas_call(
        kernel,
        out_shape=out_shape,
        in_specs=in_specs,
        out_specs=out_specs,
        scratch_shapes=list(scratch),
        compiler_params=pltpu.CompilerParams(vmem_limit_bytes=LIMIT),
        cost_estimate=pl.CostEstimate(flops=flops, bytes_accessed=nbytes, transcendentals=0),
    )


def spread_kernel(w_ref, out_ref):
    count, width = w_ref.shape
    weight = w_ref[...].astype(F32)
    pieces = [weight[:, j * LANES : (j + 1) * LANES] for j in range(width // LANES)]
    rows = jnp.concatenate(pieces, axis=0).astype(BF16)
    for chunk in range(out_ref.shape[0]):
        out_ref[chunk] = rows


def pack_kernel(q_hbm, k_hbm, v_hbm, out_ref, rows_ref, sems):
    heads = out_ref.shape[0]
    copies = [
        pltpu.make_async_copy(source, rows_ref.at[i], sems.at[i])
        for i, source in enumerate((q_hbm, k_hbm, v_hbm))
    ]
    for copy in copies:
        copy.start()
    for i, copy in enumerate(copies):
        copy.wait()
        for pair in range(heads // 2):
            both = rows_ref[i, :, pair * 2 * DH : (pair + 1) * 2 * DH].T
            out_ref[2 * pair, i * DH : (i + 1) * DH, :] = both[:DH]
            out_ref[2 * pair + 1, i * DH : (i + 1) * DH, :] = both[DH:]


def unpack_kernel(x_ref, q_ref, k_ref, v_ref, proj_ref):
    for pair in range(x_ref.shape[0] // 2):
        for i, out_ref in enumerate((q_ref, k_ref, v_ref)):
            rows = slice(i * DH, (i + 1) * DH)
            both = jnp.concatenate([x_ref[2 * pair, rows, :], x_ref[2 * pair + 1, rows, :]], axis=0)
            out_ref[:, pair * 2 * DH : (pair + 1) * 2 * DH] = both.T
    for row, col, chunk in proj_tiles(proj_ref.shape):
        proj_ref[row, col] = x_ref[chunk, 3 * DH :, :].astype(F32)


def proj_tiles(shape):
    rows, width = shape
    per_row = width // LANES
    for i in range(rows // SUM_ROWS):
        for j in range(per_row):
            yield (
                slice(i * SUM_ROWS, (i + 1) * SUM_ROWS),
                slice(j * LANES, (j + 1) * LANES),
                i * per_row + j,
            )


def user_edges(len_ref):
    ends = []
    total = 0
    for i in range(len_ref.shape[1]):
        total = total + len_ref[0, i]
        ends.append(total)
    return ends


def user_start(position, ends):
    start = jnp.zeros_like(position)
    for end in ends[:-1]:
        start = jnp.where(position >= end, end, start)
    return start


def user_inverse(position, ends, len_ref):
    length = jnp.full(position.shape, len_ref[0, 0], jnp.int32)
    for i, end in enumerate(ends[:-1]):
        length = jnp.where(position >= end, len_ref[0, i + 1], length)
    return 1.0 / length.astype(F32)


def lane_pair(ref, block, rows):
    return jnp.concatenate([ref[2 * block, rows, :], ref[2 * block + 1, rows, :]], axis=1)


def tile_allowed(diagonal, col_block, starts, positions):
    key_pos = lax.broadcasted_iota(jnp.int32, (TILE, TILE), 0)
    shift = col_block * TILE
    allowed = key_pos >= starts - shift
    return allowed & (key_pos <= positions - shift) if diagonal else allowed


def block_rows(row_block, ends):
    positions = row_block * TILE + lax.broadcasted_iota(jnp.int32, (1, TILE), 1)
    return positions, user_start(positions, ends)


def first_block(row_block, ends):
    return lax.div(user_start(row_block * TILE, ends), TILE)


def natural(source_ref, rows, target_ref):
    for block in range(target_ref.shape[0]):
        for half in range(2):
            target_ref[block, half * LANES : (half + 1) * LANES, :] = source_ref[
                2 * block + half, rows, :
            ].T


Q_ROWS = slice(0, DH)
K_ROWS = slice(DH, 2 * DH)
V_ROWS = slice(2 * DH, 3 * DH)
CONTRACT_LANES = (((1,), (1,)), ((), ()))


def gate_and_silu(raw):
    half = raw * (0.5 / math.sqrt(DH))
    gate = 0.5 * jnp.tanh(half) + 0.5
    return gate, (half + half) * gate


def row_pair(ref, pair, rows):
    return [lane_pair(ref, 2 * pair + i, rows) for i in range(2)]


def forward_kernel(len_ref, qkv_ref, out_ref, k_nat, attn_ref):
    ends = user_edges(len_ref)
    natural(qkv_ref, K_ROWS, k_nat)
    for pair in range(k_nat.shape[0] // 2):
        low, high = 2 * pair, 2 * pair + 1
        q_t = row_pair(qkv_ref, pair, Q_ROWS)
        places = [block_rows(row, ends) for row in (low, high)]
        first = first_block(low, ends)

        def score(i, col, diagonal, q_t=q_t, places=places):
            raw = jnp.dot(k_nat[col], q_t[i], preferred_element_type=F32)
            _, silu = gate_and_silu(raw)
            positions, starts = places[i]
            allowed = tile_allowed(diagonal, col, starts, positions)
            return jnp.where(allowed, silu, 0.0).astype(BF16)

        def product(col, attn):
            return jnp.dot(lane_pair(qkv_ref, col, V_ROWS), attn, preferred_element_type=F32)

        def step(i, totals, low=low, score=score):
            col = low - 1 - i
            before = attn_ref[0], attn_ref[1]
            attn_low = score(0, col, False)
            total_low = totals[0] + product(col + 1, before[0])
            attn_high = score(1, col, False)
            total_high = totals[1] + product(col + 1, before[1])
            attn_ref[0] = attn_low
            attn_ref[1] = attn_high
            return total_low, total_high

        diagonal = score(1, high, True)
        attn_ref[0] = score(0, low, True)
        totals = jnp.zeros((DH, TILE), F32), product(high, diagonal)
        attn_ref[1] = score(1, low, False)
        totals = lax.fori_loop(0, low - first, step, totals)
        for i, row in enumerate((low, high)):
            total = totals[i] + product(first, attn_ref[i])
            total = total * user_inverse(places[i][0], ends, len_ref)
            out_ref[2 * row] = total[:, :LANES].astype(BF16)
            out_ref[2 * row + 1] = total[:, LANES:].astype(BF16)


def backward_kernel(
    len_ref, qkv_ref, g_ref, out_ref, k_nat, v_nat, k_acc, v_acc, attn_ref, grad_ref
):
    blocks = v_nat.shape[0]
    scale = 1.0 / math.sqrt(DH)
    ends = user_edges(len_ref)
    natural(qkv_ref, K_ROWS, k_nat)
    natural(qkv_ref, V_ROWS, v_nat)
    k_acc[...] = jnp.zeros_like(k_acc)
    v_acc[...] = jnp.zeros_like(v_acc)
    for pair in range(blocks // 2):
        low, high = 2 * pair, 2 * pair + 1
        q_t = row_pair(qkv_ref, pair, Q_ROWS)
        g_t = row_pair(g_ref, pair, slice(0, DH))
        places = [block_rows(row, ends) for row in (low, high)]
        first = first_block(low, ends)

        def score(i, col, diagonal, q_t=q_t, g_t=g_t, places=places):
            raw = jnp.dot(k_nat[col], q_t[i], preferred_element_type=F32)
            attn_grad = jnp.dot(v_nat[col], g_t[i], preferred_element_type=F32)
            gate, silu = gate_and_silu(raw)
            score_grad = attn_grad * (gate + silu * (1.0 - gate))
            positions, starts = places[i]
            allowed = tile_allowed(diagonal, col, starts, positions)
            return (
                jnp.where(allowed, silu, 0.0).astype(BF16),
                jnp.where(allowed, score_grad, 0.0).astype(BF16),
            )

        def product(i, col, attn, score_grad, q_t=q_t, g_t=g_t):
            v_acc[col] += lax.dot_general(g_t[i], attn, CONTRACT_LANES, preferred_element_type=F32)
            k_acc[col] += lax.dot_general(
                q_t[i], score_grad, CONTRACT_LANES, preferred_element_type=F32
            )
            return jnp.dot(lane_pair(qkv_ref, col, K_ROWS), score_grad, preferred_element_type=F32)

        def keep(i, tile):
            attn_ref[i], grad_ref[i] = tile

        def kept(i):
            return attn_ref[i], grad_ref[i]

        def step(i, totals, low=low, score=score, product=product):
            col = low - 1 - i
            before = kept(0), kept(1)
            tile_low = score(0, col, False)
            total_low = totals[0] + product(0, col + 1, *before[0])
            tile_high = score(1, col, False)
            total_high = totals[1] + product(1, col + 1, *before[1])
            keep(0, tile_low)
            keep(1, tile_high)
            return total_low, total_high

        diagonal = score(1, high, True)
        keep(0, score(0, low, True))
        totals = jnp.zeros((DH, TILE), F32), product(1, high, *diagonal)
        keep(1, score(1, low, False))
        totals = lax.fori_loop(0, low - first, step, totals)
        for i, row in enumerate((low, high)):
            total = totals[i] + product(i, first, *kept(i))
            total = (total * scale).astype(BF16)
            out_ref[2 * row, 0:DH, :] = total[:, :LANES]
            out_ref[2 * row + 1, 0:DH, :] = total[:, LANES:]
    total = jnp.sum(g_ref[:, DH:, :].astype(F32), axis=0).astype(BF16)
    for chunk in range(out_ref.shape[0]):
        out_ref[chunk, 3 * DH :, :] = total
    for block in range(blocks):
        k_grad = (k_acc[block] * scale).astype(BF16)
        v_grad = v_acc[block].astype(BF16)
        for half in range(2):
            lanes = slice(half * LANES, (half + 1) * LANES)
            out_ref[2 * block + half, DH : 2 * DH, :] = k_grad[:, lanes]
            out_ref[2 * block + half, 2 * DH : 3 * DH, :] = v_grad[:, lanes]


def project_kernel(
    place_ref, w0_ref, w1_ref, w2_low_ref, w2_high_ref, w3_ref, out_grad_ref, other_grad_ref, mine_ref, theirs_ref
):
    side, rows, width = w0_ref.shape
    tokens = out_grad_ref.shape[0]
    both = jnp.concatenate([out_grad_ref[...], other_grad_ref[...]], axis=0)
    pieces = [(w0_ref, 0, 0), (w1_ref, 1, 0), (w2_low_ref, 2, 0), (w2_high_ref, 2, side // 2), (w3_ref, 3, 0)]
    for ref, y_back, x_first in pieces:
        count = ref.shape[0]
        product = lax.dot_general(
            ref[...].reshape(count * rows, width), both, CONTRACT_LANES, preferred_element_type=F32
        )
        y = lax.rem(place_ref[3] + side - y_back, side)
        for i in range(count):
            x = lax.rem(place_ref[2] + side - x_first - i, side)
            mine_ref[x * side + y] = product[i * rows : (i + 1) * rows, :tokens]
            theirs_ref[x * side + y] = product[i * rows : (i + 1) * rows, tokens:]


def norm_stats(o_ref):
    heads, _, tokens = o_ref.shape
    share = 1.0 / (heads * DH)
    total = jnp.zeros((DH, tokens), F32)
    for head in range(heads):
        total = total + o_ref[head].astype(F32)
    mean = jnp.sum(total, axis=0, keepdims=True) * share
    total = jnp.zeros((DH, tokens), F32)
    for head in range(heads):
        centred = o_ref[head].astype(F32) - mean
        total = total + centred * centred
    var = jnp.sum(total, axis=0, keepdims=True) * share
    return mean, lax.rsqrt(var + 1e-05)


def gated_kernel(place_ref, o_ref, gate_ref, mine_ref, other_ref):
    half = DH // 2
    even = place_ref[1] == 0
    mean, rstd = norm_stats(o_ref)
    for pair in range(o_ref.shape[0] // 2):
        gates = gate_ref[:, pair * 2 * DH : (pair + 1) * 2 * DH].T.astype(F32)
        for i in range(2):
            head = 2 * pair + i
            normed = (o_ref[head].astype(F32) - mean) * rstd
            gated = normed * gates[i * DH : (i + 1) * DH]
            low, high = gated[:half], gated[half:]
            mine_ref[head] = jnp.where(even, low, high).astype(BF16)
            other_ref[head] = jnp.where(even, high, low).astype(BF16)


def norm_kernel(
    len_ref, place_ref, o_ref, mine_ref, recv_ref, gate_ref, grad_ref, gate_grad_ref, normed_grad_ref
):
    heads, _, tokens = o_ref.shape
    width = heads * DH
    even = place_ref[1] == 0
    mean, rstd = norm_stats(o_ref)
    first = jnp.zeros((DH, tokens), F32)
    second = jnp.zeros((DH, tokens), F32)
    for pair in range(heads // 2):
        cols = slice(pair * 2 * DH, (pair + 1) * 2 * DH)
        gates = gate_ref[:, cols].T.astype(F32)
        gate_grads = []
        for i in range(2):
            head = 2 * pair + i
            normed = (o_ref[head].astype(F32) - mean) * rstd
            mine, recv = mine_ref[head], recv_ref[head]
            gated_grad = jnp.concatenate(
                [jnp.where(even, mine, recv), jnp.where(even, recv, mine)], axis=0
            )
            gate_grads.append((gated_grad * normed).astype(BF16))
            normed_grad = gated_grad * gates[i * DH : (i + 1) * DH]
            first = first + normed_grad
            second = second + normed_grad * normed
            normed_grad_ref[head] = normed_grad
        gate_grad_ref[:, cols] = jnp.concatenate(gate_grads, axis=0).T
    first = jnp.sum(first, axis=0, keepdims=True) * (1.0 / width)
    second = jnp.sum(second, axis=0, keepdims=True) * (1.0 / width)
    position = place_ref[0] * tokens + lax.broadcasted_iota(jnp.int32, (1, tokens), 1)
    weight = rstd * user_inverse(position, user_edges(len_ref), len_ref)
    for head in range(heads):
        normed = (o_ref[head].astype(F32) - mean) * rstd
        grad_ref[head] = ((normed_grad_ref[head] - first - normed * second) * weight).astype(BF16)


def proj_kernel(mine_ref, other_ref, out_grad_ref, other_grad_ref, out_ref):
    chips, rows, width = out_ref.shape
    tokens = out_grad_ref.shape[0]
    step = 8
    for i in range(chips // step):
        part = slice(i * step, (i + 1) * step)
        mine = mine_ref[part].reshape(step * rows, tokens)
        other = other_ref[part].reshape(step * rows, tokens)
        left = jnp.concatenate([mine, other], axis=1)
        for j in range(width // 256):
            cols = slice(j * 256, (j + 1) * 256)
            right = jnp.concatenate([out_grad_ref[:, cols], other_grad_ref[:, cols]], axis=0)
            product = jnp.dot(left, right, preferred_element_type=F32)
            out_ref[part, :, cols] = product.astype(BF16).reshape(step, rows, 256)


def sum_kernel(x_ref, grad_ref, out_ref):
    _, rows, width = x_ref.shape
    out_ref[:, :DH, :] = grad_ref[...]
    for row, col, chunk in proj_tiles((rows, width)):
        tile = jnp.sum(x_ref[:, row, col].astype(F32), axis=0)
        out_ref[chunk, DH:, :] = tile.astype(BF16)


def exchange(array, axis, groups=None):
    return lax.all_to_all(
        array, axis, split_axis=0, concat_axis=0, tiled=True, axis_index_groups=groups
    )


SIDE = 4


def plane_shift(axis, step):
    moves = []
    for i in range(2 * SIDE * SIDE):
        x, y, core = i // (2 * SIDE), i // 2 % SIDE, i % 2
        if axis == "x":
            x = (x + step) % SIDE
        else:
            y = (y + step) % SIDE
        moves.append((i, (x * SIDE + y) * 2 + core))
    return moves


def ring_near(block, axis):
    return tuple(lax.ppermute(block, "dp", plane_shift(axis, step)) for step in (1, -1))


def ring_far(back_one, back_three, axis):
    half = back_one.shape[0] // 2
    low = lax.ppermute(back_one[:half], "dp", plane_shift(axis, 1))
    high = lax.ppermute(back_three[half:], "dp", plane_shift(axis, -1))
    return low, high


def ring_blocks(block, axis):
    back_one, back_three = ring_near(block, axis)
    return (block, back_one) + ring_far(back_one, back_three, axis) + (back_three,)


def local(query_rows, key_rows, value_rows, gate_rows, out_grad, proj_weight, user_lengths):
    ctx = lax.axis_size("ctx")
    dp = lax.axis_size("dp")
    tokens, width = query_rows.shape
    heads = width // DH
    group = tokens * ctx
    blocks = group // TILE
    chips = dp // 2
    out_rows = width // dp
    w_rows = proj_weight.size // LANES
    shape = jax.ShapeDtypeStruct
    partner = [(i, i ^ 1) for i in range(dp)]
    same_core = [[2 * i + core for i in range(chips)] for core in range(2)]
    chip = lax.axis_index("dp") // 2
    place = jnp.stack(
        [lax.axis_index("ctx"), lax.rem(lax.axis_index("dp"), 2), chip // SIDE, lax.rem(chip, SIDE)]
    ).astype(jnp.int32)
    in_hbm = pl.BlockSpec(memory_space=pltpu.HBM)

    block = call(
        spread_kernel, shape((ctx, w_rows, LANES), BF16), [VMEM], nbytes=tokens * width
    )(proj_weight)
    block = exchange(block, "ctx")
    qkv = call(
        pack_kernel,
        shape((heads, 3 * DH, tokens), BF16),
        [in_hbm] * 3,
        [pltpu.VMEM((3, tokens, width), BF16), pltpu.SemaphoreType.DMA((3,))],
        nbytes=6 * tokens * width * 2,
    )(query_rows, key_rows, value_rows)
    block, qkv = lax.optimization_barrier((block, qkv))
    qkv = exchange(qkv, "ctx")

    block = block.reshape(ctx, width // LANES, out_rows // ctx, LANES).transpose(0, 2, 1, 3)
    block = block.reshape(out_rows, width)
    column = jnp.concatenate(ring_blocks(block, "x"), axis=0).reshape(SIDE, out_rows, width)
    column, own_grad = lax.optimization_barrier((column, out_grad))
    near = ring_near(column, "y")
    other_grad = lax.ppermute(own_grad, "dp", partner)
    qkv, near, other_grad = lax.optimization_barrier((qkv, near, other_grad))
    far = ring_far(*near, "y")
    attn_out = call(
        forward_kernel,
        shape((ctx, DH, tokens), BF16),
        [SMEM, VMEM],
        [pltpu.VMEM((blocks, TILE, DH), BF16), pltpu.VMEM((2, TILE, TILE), BF16)],
        flops=group * group * DH * 2,
        nbytes=5 * group * DH * 2,
    )(user_lengths, qkv)
    attn_out = exchange(attn_out, "ctx")
    attn_out, far = lax.optimization_barrier((attn_out, far))

    mine, theirs = call(
        project_kernel,
        [shape((heads, DH // 2, tokens), F32)] * 2,
        [SMEM] + [VMEM] * 7,
        flops=2 * tokens * width * width,
        nbytes=2 * width * width,
    )(place, column, near[0], *far, near[1], out_grad, other_grad)
    received = lax.ppermute(theirs, "dp", partner)

    gated_mine, gated_other = call(
        gated_kernel,
        [shape((heads, DH // 2, tokens), BF16)] * 2,
        [SMEM, VMEM, VMEM],
        nbytes=6 * tokens * width,
    )(place, attn_out, gate_rows)
    other = lax.ppermute(gated_other, "dp", partner)
    partial = call(
        proj_kernel,
        shape((chips, out_rows, width), BF16),
        [VMEM] * 4,
        flops=2 * tokens * width * width,
        nbytes=2 * width * width,
    )(gated_mine, other, out_grad, other_grad)
    partial = exchange(partial, "dp", same_core)
    grad, gate_grad = call(
        norm_kernel,
        [shape((heads, DH, tokens), BF16), shape((tokens, width), BF16)],
        [SMEM, SMEM, VMEM, VMEM, VMEM, VMEM],
        [pltpu.VMEM((heads, DH, tokens), F32)],
        nbytes=18 * tokens * width,
    )(user_lengths, place, attn_out, mine, received, gate_rows)
    grad = call(
        sum_kernel,
        shape((ctx, DH + w_rows, tokens), BF16),
        [VMEM, VMEM],
        nbytes=width * width + 4 * tokens * width,
    )(partial, grad)
    grad = exchange(grad, "ctx")

    grads = call(
        backward_kernel,
        shape((ctx, 3 * DH + w_rows, tokens), BF16),
        [SMEM, VMEM, VMEM],
        [
            pltpu.VMEM((blocks, TILE, DH), BF16),
            pltpu.VMEM((blocks, TILE, DH), BF16),
            pltpu.VMEM((blocks, DH, TILE), F32),
            pltpu.VMEM((blocks, DH, TILE), F32),
            pltpu.VMEM((2, TILE, TILE), BF16),
            pltpu.VMEM((2, TILE, TILE), BF16),
        ],
        flops=3 * group * group * DH * 2,
        nbytes=7 * group * DH * 2,
    )(user_lengths, qkv, grad)
    grads = exchange(grads, "ctx")
    query_grad, key_grad, value_grad, proj_grad = call(
        unpack_kernel,
        [shape((tokens, width), BF16)] * 3 + [shape((out_rows, width), F32)],
        [VMEM],
        nbytes=6 * tokens * width * 2,
    )(grads)
    return (query_grad, key_grad, value_grad, gate_grad, proj_grad)


def solution(mesh):
    rows = P(("dp", "ctx"), None)
    in_specs = (rows,) * 6 + (P("dp", None),)
    out_specs = (rows,) * 4 + (P("dp", None),)
    return jax.shard_map(local, mesh=mesh, in_specs=in_specs, out_specs=out_specs, check_vma=False)
```

```python
import math

import jax
import jax.numpy as jnp
from jax import lax
from jax.experimental import pallas as pl
from jax.experimental.pallas import tpu as pltpu
from jax.sharding import PartitionSpec as P

DH = 64
LANES = 128
TILE = 256
SUM_ROWS = 16
BF16 = jnp.bfloat16
F32 = jnp.float32
VMEM = pl.BlockSpec(memory_space=pltpu.VMEM)
SMEM = pl.BlockSpec(memory_space=pltpu.SMEM)
LIMIT = 16 * 1024 * 1024


def call(kernel, out_shape, in_specs, scratch=(), flops=0, nbytes=0):
    single = not isinstance(out_shape, (list, tuple))
    out_specs = VMEM if single else [VMEM] * len(out_shape)
    return pl.pallas_call(
        kernel,
        out_shape=out_shape,
        in_specs=in_specs,
        out_specs=out_specs,
        scratch_shapes=list(scratch),
        compiler_params=pltpu.CompilerParams(vmem_limit_bytes=LIMIT),
        cost_estimate=pl.CostEstimate(flops=flops, bytes_accessed=nbytes, transcendentals=0),
    )


def spread_kernel(w_ref, out_ref):
    count, width = w_ref.shape
    weight = w_ref[...].astype(F32)
    pieces = [weight[:, j * LANES : (j + 1) * LANES] for j in range(width // LANES)]
    rows = jnp.concatenate(pieces, axis=0).astype(BF16)
    for chunk in range(out_ref.shape[0]):
        out_ref[chunk] = rows


def pack_kernel(q_hbm, k_hbm, v_hbm, out_ref, rows_ref, sems):
    heads = out_ref.shape[0]
    copies = [
        pltpu.make_async_copy(source, rows_ref.at[i], sems.at[i])
        for i, source in enumerate((q_hbm, k_hbm, v_hbm))
    ]
    for copy in copies:
        copy.start()
    for i, copy in enumerate(copies):
        copy.wait()
        for pair in range(heads // 2):
            both = rows_ref[i, :, pair * 2 * DH : (pair + 1) * 2 * DH].T
            out_ref[2 * pair, i * DH : (i + 1) * DH, :] = both[:DH]
            out_ref[2 * pair + 1, i * DH : (i + 1) * DH, :] = both[DH:]


def unpack_kernel(x_ref, q_ref, k_ref, v_ref, proj_ref):
    for pair in range(x_ref.shape[0] // 2):
        for i, out_ref in enumerate((q_ref, k_ref, v_ref)):
            rows = slice(i * DH, (i + 1) * DH)
            both = jnp.concatenate([x_ref[2 * pair, rows, :], x_ref[2 * pair + 1, rows, :]], axis=0)
            out_ref[:, pair * 2 * DH : (pair + 1) * 2 * DH] = both.T
    for row, col, chunk in proj_tiles(proj_ref.shape):
        proj_ref[row, col] = x_ref[chunk, 3 * DH :, :].astype(F32)


def proj_tiles(shape):
    rows, width = shape
    per_row = width // LANES
    for i in range(rows // SUM_ROWS):
        for j in range(per_row):
            yield (
                slice(i * SUM_ROWS, (i + 1) * SUM_ROWS),
                slice(j * LANES, (j + 1) * LANES),
                i * per_row + j,
            )


PLACE = 4


def place_of(info_ref, i):
    return info_ref[info_ref.shape[0] - PLACE + i]


def user_edges(info_ref):
    ends = []
    total = 0
    for i in range(info_ref.shape[0] - PLACE):
        total = total + info_ref[i]
        ends.append(total)
    return ends


def user_start(position, ends):
    start = jnp.zeros_like(position)
    for end in ends[:-1]:
        start = jnp.where(position >= end, end, start)
    return start


def user_inverse(position, ends, info_ref):
    length = jnp.full(position.shape, info_ref[0], jnp.int32)
    for i, end in enumerate(ends[:-1]):
        length = jnp.where(position >= end, info_ref[i + 1], length)
    return 1.0 / length.astype(F32)


def lane_pair(ref, block, rows):
    return jnp.concatenate([ref[2 * block, rows, :], ref[2 * block + 1, rows, :]], axis=1)


def tile_allowed(diagonal, col_block, starts, positions):
    key_pos = lax.broadcasted_iota(jnp.int32, (TILE, TILE), 0)
    shift = col_block * TILE
    allowed = key_pos >= starts - shift
    return allowed & (key_pos <= positions - shift) if diagonal else allowed


def block_rows(row_block, ends):
    positions = row_block * TILE + lax.broadcasted_iota(jnp.int32, (1, TILE), 1)
    return positions, user_start(positions, ends)


def first_block(row_block, ends):
    return lax.div(user_start(row_block * TILE, ends), TILE)


def natural(source_ref, rows, target_ref):
    for block in range(target_ref.shape[0]):
        for half in range(2):
            target_ref[block, half * LANES : (half + 1) * LANES, :] = source_ref[
                2 * block + half, rows, :
            ].T


Q_ROWS = slice(0, DH)
K_ROWS = slice(DH, 2 * DH)
V_ROWS = slice(2 * DH, 3 * DH)
CONTRACT_LANES = (((1,), (1,)), ((), ()))


def gate_and_silu(raw):
    half = raw * (0.5 / math.sqrt(DH))
    gate = 0.5 * jnp.tanh(half) + 0.5
    return gate, (half + half) * gate


def row_pair(ref, pair, rows):
    return [lane_pair(ref, 2 * pair + i, rows) for i in range(2)]


def forward_kernel(info_ref, qkv_ref, out_ref, k_nat, attn_ref):
    ends = user_edges(info_ref)
    natural(qkv_ref, K_ROWS, k_nat)
    for pair in range(k_nat.shape[0] // 2):
        low, high = 2 * pair, 2 * pair + 1
        q_t = row_pair(qkv_ref, pair, Q_ROWS)
        places = [block_rows(row, ends) for row in (low, high)]
        first = first_block(low, ends)

        def score(i, col, diagonal, q_t=q_t, places=places):
            raw = jnp.dot(k_nat[col], q_t[i], preferred_element_type=F32)
            _, silu = gate_and_silu(raw)
            positions, starts = places[i]
            allowed = tile_allowed(diagonal, col, starts, positions)
            return jnp.where(allowed, silu, 0.0).astype(BF16)

        def product(col, attn):
            return jnp.dot(lane_pair(qkv_ref, col, V_ROWS), attn, preferred_element_type=F32)

        def step(i, totals, low=low, score=score):
            col = low - 1 - i
            before = attn_ref[0], attn_ref[1]
            attn_low = score(0, col, False)
            total_low = totals[0] + product(col + 1, before[0])
            attn_high = score(1, col, False)
            total_high = totals[1] + product(col + 1, before[1])
            attn_ref[0] = attn_low
            attn_ref[1] = attn_high
            return total_low, total_high

        diagonal = score(1, high, True)
        attn_ref[0] = score(0, low, True)
        totals = jnp.zeros((DH, TILE), F32), product(high, diagonal)
        attn_ref[1] = score(1, low, False)
        totals = lax.fori_loop(0, low - first, step, totals)
        for i, row in enumerate((low, high)):
            total = totals[i] + product(first, attn_ref[i])
            total = total * user_inverse(places[i][0], ends, info_ref)
            out_ref[2 * row] = total[:, :LANES].astype(BF16)
            out_ref[2 * row + 1] = total[:, LANES:].astype(BF16)


def backward_kernel(
    info_ref, qkv_ref, g_ref, out_ref, k_nat, v_nat, k_acc, v_acc, attn_ref, grad_ref
):
    blocks = v_nat.shape[0]
    scale = 1.0 / math.sqrt(DH)
    ends = user_edges(info_ref)
    natural(qkv_ref, K_ROWS, k_nat)
    natural(qkv_ref, V_ROWS, v_nat)
    k_acc[...] = jnp.zeros_like(k_acc)
    v_acc[...] = jnp.zeros_like(v_acc)
    for pair in range(blocks // 2):
        low, high = 2 * pair, 2 * pair + 1
        q_t = row_pair(qkv_ref, pair, Q_ROWS)
        g_t = row_pair(g_ref, pair, slice(0, DH))
        places = [block_rows(row, ends) for row in (low, high)]
        first = first_block(low, ends)

        def score(i, col, diagonal, q_t=q_t, g_t=g_t, places=places):
            raw = jnp.dot(k_nat[col], q_t[i], preferred_element_type=F32)
            attn_grad = jnp.dot(v_nat[col], g_t[i], preferred_element_type=F32)
            gate, silu = gate_and_silu(raw)
            score_grad = attn_grad * (gate + silu * (1.0 - gate))
            positions, starts = places[i]
            allowed = tile_allowed(diagonal, col, starts, positions)
            return (
                jnp.where(allowed, silu, 0.0).astype(BF16),
                jnp.where(allowed, score_grad, 0.0).astype(BF16),
            )

        def product(i, col, attn, score_grad, q_t=q_t, g_t=g_t):
            v_acc[col] += lax.dot_general(g_t[i], attn, CONTRACT_LANES, preferred_element_type=F32)
            k_acc[col] += lax.dot_general(
                q_t[i], score_grad, CONTRACT_LANES, preferred_element_type=F32
            )
            return jnp.dot(lane_pair(qkv_ref, col, K_ROWS), score_grad, preferred_element_type=F32)

        def keep(i, tile):
            attn_ref[i], grad_ref[i] = tile

        def kept(i):
            return attn_ref[i], grad_ref[i]

        def step(i, totals, low=low, score=score, product=product):
            col = low - 1 - i
            before = kept(0), kept(1)
            tile_low = score(0, col, False)
            total_low = totals[0] + product(0, col + 1, *before[0])
            tile_high = score(1, col, False)
            total_high = totals[1] + product(1, col + 1, *before[1])
            keep(0, tile_low)
            keep(1, tile_high)
            return total_low, total_high

        diagonal = score(1, high, True)
        keep(0, score(0, low, True))
        totals = jnp.zeros((DH, TILE), F32), product(1, high, *diagonal)
        keep(1, score(1, low, False))
        totals = lax.fori_loop(0, low - first, step, totals)
        for i, row in enumerate((low, high)):
            total = totals[i] + product(i, first, *kept(i))
            total = (total * scale).astype(BF16)
            out_ref[2 * row, 0:DH, :] = total[:, :LANES]
            out_ref[2 * row + 1, 0:DH, :] = total[:, LANES:]
    total = jnp.sum(g_ref[:, DH:, :].astype(F32), axis=0).astype(BF16)
    for chunk in range(out_ref.shape[0]):
        out_ref[chunk, 3 * DH :, :] = total
    for block in range(blocks):
        k_grad = (k_acc[block] * scale).astype(BF16)
        v_grad = v_acc[block].astype(BF16)
        for half in range(2):
            lanes = slice(half * LANES, (half + 1) * LANES)
            out_ref[2 * block + half, DH : 2 * DH, :] = k_grad[:, lanes]
            out_ref[2 * block + half, 2 * DH : 3 * DH, :] = v_grad[:, lanes]


def project_kernel(
    info_ref, w0_ref, w1_ref, w2_low_ref, w2_high_ref, w3_ref, out_grad_ref, other_grad_ref, mine_ref, theirs_ref
):
    side, rows, width = w0_ref.shape
    tokens = out_grad_ref.shape[0]
    both = jnp.concatenate([out_grad_ref[...], other_grad_ref[...]], axis=0)
    pieces = [(w0_ref, 0, 0), (w1_ref, 1, 0), (w2_low_ref, 2, 0), (w2_high_ref, 2, side // 2), (w3_ref, 3, 0)]
    for ref, y_back, x_first in pieces:
        count = ref.shape[0]
        product = lax.dot_general(
            ref[...].reshape(count * rows, width), both, CONTRACT_LANES, preferred_element_type=F32
        )
        y = lax.rem(place_of(info_ref, 3) + side - y_back, side)
        for i in range(count):
            x = lax.rem(place_of(info_ref, 2) + side - x_first - i, side)
            mine_ref[x * side + y] = product[i * rows : (i + 1) * rows, :tokens]
            theirs_ref[x * side + y] = product[i * rows : (i + 1) * rows, tokens:]


def norm_stats(o_ref):
    heads, _, tokens = o_ref.shape
    share = 1.0 / (heads * DH)
    total = jnp.zeros((DH, tokens), F32)
    for head in range(heads):
        total = total + o_ref[head].astype(F32)
    mean = jnp.sum(total, axis=0, keepdims=True) * share
    total = jnp.zeros((DH, tokens), F32)
    for head in range(heads):
        centred = o_ref[head].astype(F32) - mean
        total = total + centred * centred
    var = jnp.sum(total, axis=0, keepdims=True) * share
    return mean, lax.rsqrt(var + 1e-05)


def gated_kernel(info_ref, o_ref, gate_ref, mine_ref, other_ref):
    half = DH // 2
    even = place_of(info_ref, 1) == 0
    mean, rstd = norm_stats(o_ref)
    for pair in range(o_ref.shape[0] // 2):
        gates = gate_ref[:, pair * 2 * DH : (pair + 1) * 2 * DH].T.astype(F32)
        for i in range(2):
            head = 2 * pair + i
            normed = (o_ref[head].astype(F32) - mean) * rstd
            gated = normed * gates[i * DH : (i + 1) * DH]
            low, high = gated[:half], gated[half:]
            mine_ref[head] = jnp.where(even, low, high).astype(BF16)
            other_ref[head] = jnp.where(even, high, low).astype(BF16)


def norm_kernel(
    info_ref, o_ref, mine_ref, recv_ref, gate_ref, grad_ref, gate_grad_ref, normed_grad_ref
):
    heads, _, tokens = o_ref.shape
    width = heads * DH
    even = place_of(info_ref, 1) == 0
    mean, rstd = norm_stats(o_ref)
    first = jnp.zeros((DH, tokens), F32)
    second = jnp.zeros((DH, tokens), F32)
    for pair in range(heads // 2):
        cols = slice(pair * 2 * DH, (pair + 1) * 2 * DH)
        gates = gate_ref[:, cols].T.astype(F32)
        gate_grads = []
        for i in range(2):
            head = 2 * pair + i
            normed = (o_ref[head].astype(F32) - mean) * rstd
            mine, recv = mine_ref[head], recv_ref[head]
            gated_grad = jnp.concatenate(
                [jnp.where(even, mine, recv), jnp.where(even, recv, mine)], axis=0
            )
            gate_grads.append((gated_grad * normed).astype(BF16))
            normed_grad = gated_grad * gates[i * DH : (i + 1) * DH]
            first = first + normed_grad
            second = second + normed_grad * normed
            normed_grad_ref[head] = normed_grad
        gate_grad_ref[:, cols] = jnp.concatenate(gate_grads, axis=0).T
    first = jnp.sum(first, axis=0, keepdims=True) * (1.0 / width)
    second = jnp.sum(second, axis=0, keepdims=True) * (1.0 / width)
    position = place_of(info_ref, 0) * tokens + lax.broadcasted_iota(jnp.int32, (1, tokens), 1)
    weight = rstd * user_inverse(position, user_edges(info_ref), info_ref)
    for head in range(heads):
        normed = (o_ref[head].astype(F32) - mean) * rstd
        grad_ref[head] = ((normed_grad_ref[head] - first - normed * second) * weight).astype(BF16)


def proj_kernel(mine_ref, other_ref, out_grad_ref, other_grad_ref, out_ref):
    chips, rows, width = out_ref.shape
    tokens = out_grad_ref.shape[0]
    step = 8
    for i in range(chips // step):
        part = slice(i * step, (i + 1) * step)
        mine = mine_ref[part].reshape(step * rows, tokens)
        other = other_ref[part].reshape(step * rows, tokens)
        left = jnp.concatenate([mine, other], axis=1)
        for j in range(width // 256):
            cols = slice(j * 256, (j + 1) * 256)
            right = jnp.concatenate([out_grad_ref[:, cols], other_grad_ref[:, cols]], axis=0)
            product = jnp.dot(left, right, preferred_element_type=F32)
            out_ref[part, :, cols] = product.astype(BF16).reshape(step, rows, 256)


def sum_kernel(x_ref, grad_ref, out_ref):
    _, rows, width = x_ref.shape
    out_ref[:, :DH, :] = grad_ref[...]
    for row, col, chunk in proj_tiles((rows, width)):
        tile = jnp.sum(x_ref[:, row, col].astype(F32), axis=0)
        out_ref[chunk, DH:, :] = tile.astype(BF16)


def exchange(array, axis, groups=None):
    return lax.all_to_all(
        array, axis, split_axis=0, concat_axis=0, tiled=True, axis_index_groups=groups
    )


SIDE = 4


def plane_shift(axis, step):
    moves = []
    for i in range(2 * SIDE * SIDE):
        x, y, core = i // (2 * SIDE), i // 2 % SIDE, i % 2
        if axis == "x":
            x = (x + step) % SIDE
        else:
            y = (y + step) % SIDE
        moves.append((i, (x * SIDE + y) * 2 + core))
    return moves


def ring_near(block, axis):
    return tuple(lax.ppermute(block, "dp", plane_shift(axis, step)) for step in (1, -1))


def ring_far(back_one, back_three, axis):
    half = back_one.shape[0] // 2
    low = lax.ppermute(back_one[:half], "dp", plane_shift(axis, 1))
    high = lax.ppermute(back_three[half:], "dp", plane_shift(axis, -1))
    return low, high


def local(query_rows, key_rows, value_rows, gate_rows, out_grad, proj_weight, user_lengths):
    ctx = lax.axis_size("ctx")
    dp = lax.axis_size("dp")
    tokens, width = query_rows.shape
    heads = width // DH
    group = tokens * ctx
    blocks = group // TILE
    chips = dp // 2
    out_rows = width // dp
    w_rows = proj_weight.size // LANES
    shape = jax.ShapeDtypeStruct
    partner = [(i, i ^ 1) for i in range(dp)]
    same_core = [[2 * i + core for i in range(chips)] for core in range(2)]
    chip = lax.axis_index("dp") // 2
    place = [lax.axis_index("ctx"), lax.rem(lax.axis_index("dp"), 2), chip // SIDE, lax.rem(chip, SIDE)]
    info = jnp.concatenate([user_lengths[0], jnp.stack(place).astype(jnp.int32)])
    in_hbm = pl.BlockSpec(memory_space=pltpu.HBM)

    block = call(
        spread_kernel, shape((ctx, w_rows, LANES), BF16), [VMEM], nbytes=tokens * width
    )(proj_weight)
    block = exchange(block, "ctx")
    qkv = call(
        pack_kernel,
        shape((heads, 3 * DH, tokens), BF16),
        [in_hbm] * 3,
        [pltpu.VMEM((3, tokens, width), BF16), pltpu.SemaphoreType.DMA((3,))],
        nbytes=6 * tokens * width * 2,
    )(query_rows, key_rows, value_rows)
    block, qkv = lax.optimization_barrier((block, qkv))
    qkv = exchange(qkv, "ctx")

    block = block.reshape(ctx, width // LANES, out_rows // ctx, LANES).transpose(0, 2, 1, 3)
    block = block.reshape(out_rows, width)
    column = [block] + [
        lax.ppermute(block, "dp", plane_shift("x", step)) for step in range(1, SIDE)
    ]
    column = jnp.concatenate(column, axis=0).reshape(SIDE, out_rows, width)
    column, own_grad = lax.optimization_barrier((column, out_grad))
    near = ring_near(column, "y")
    other_grad = lax.ppermute(own_grad, "dp", partner)
    qkv, near, other_grad = lax.optimization_barrier((qkv, near, other_grad))
    far = ring_far(*near, "y")
    attn_out = call(
        forward_kernel,
        shape((ctx, DH, tokens), BF16),
        [SMEM, VMEM],
        [pltpu.VMEM((blocks, TILE, DH), BF16), pltpu.VMEM((2, TILE, TILE), BF16)],
        flops=group * group * DH * 2,
        nbytes=5 * group * DH * 2,
    )(info, qkv)
    attn_out = exchange(attn_out, "ctx")
    attn_out, far = lax.optimization_barrier((attn_out, far))

    mine, theirs = call(
        project_kernel,
        [shape((heads, DH // 2, tokens), F32)] * 2,
        [SMEM] + [VMEM] * 7,
        flops=2 * tokens * width * width,
        nbytes=2 * width * width,
    )(info, column, near[0], *far, near[1], out_grad, other_grad)
    received = lax.ppermute(theirs, "dp", partner)

    gated_mine, gated_other = call(
        gated_kernel,
        [shape((heads, DH // 2, tokens), BF16)] * 2,
        [SMEM, VMEM, VMEM],
        nbytes=6 * tokens * width,
    )(info, attn_out, gate_rows)
    other = lax.ppermute(gated_other, "dp", partner)
    partial = call(
        proj_kernel,
        shape((chips, out_rows, width), BF16),
        [VMEM] * 4,
        flops=2 * tokens * width * width,
        nbytes=2 * width * width,
    )(gated_mine, other, out_grad, other_grad)
    partial = exchange(partial, "dp", same_core)
    grad, gate_grad = call(
        norm_kernel,
        [shape((heads, DH, tokens), BF16), shape((tokens, width), BF16)],
        [SMEM, VMEM, VMEM, VMEM, VMEM],
        [pltpu.VMEM((heads, DH, tokens), F32)],
        nbytes=18 * tokens * width,
    )(info, attn_out, mine, received, gate_rows)
    grad = call(
        sum_kernel,
        shape((ctx, DH + w_rows, tokens), BF16),
        [VMEM, VMEM],
        nbytes=width * width + 4 * tokens * width,
    )(partial, grad)
    grad = exchange(grad, "ctx")

    grads = call(
        backward_kernel,
        shape((ctx, 3 * DH + w_rows, tokens), BF16),
        [SMEM, VMEM, VMEM],
        [
            pltpu.VMEM((blocks, TILE, DH), BF16),
            pltpu.VMEM((blocks, TILE, DH), BF16),
            pltpu.VMEM((blocks, DH, TILE), F32),
            pltpu.VMEM((blocks, DH, TILE), F32),
            pltpu.VMEM((2, TILE, TILE), BF16),
            pltpu.VMEM((2, TILE, TILE), BF16),
        ],
        flops=3 * group * group * DH * 2,
        nbytes=7 * group * DH * 2,
    )(info, qkv, grad)
    grads = exchange(grads, "ctx")
    query_grad, key_grad, value_grad, proj_grad = call(
        unpack_kernel,
        [shape((tokens, width), BF16)] * 3 + [shape((out_rows, width), F32)],
        [VMEM],
        nbytes=6 * tokens * width * 2,
    )(grads)
    return (query_grad, key_grad, value_grad, gate_grad, proj_grad)


def solution(mesh):
    rows = P(("dp", "ctx"), None)
    in_specs = (rows,) * 6 + (P("dp", None),)
    out_specs = (rows,) * 4 + (P("dp", None),)
    return jax.shard_map(local, mesh=mesh, in_specs=in_specs, out_specs=out_specs, check_vma=False)
```
